512 devices in a mesh: sub: 512 (over z, y, x, core).
Axes of the slice: x: 4, y: 8, z: 8, core: 2. Of those that a mesh axis runs over, the one named last changes fastest.
Arguments:
- deflation: bfloat16 [524288, 128], P('sub'), may hold values from -0.1875 to 0.1875
- op_tiles: bfloat16 [24576, 128, 128], P('sub'), may hold values from -0.21875 to 0.21875
- tile_cols: int32 [24576], P('sub'), may hold values from 0 to 7
- diag_coef: float32 [524288], P('sub'), may hold values from 1 to 4
- fine_rhs: bfloat16 [524288, 128], P('sub'), may hold values from -6 to 6
- adjacency: int32 [512, 8], P('sub'), may hold values from 0 to 1, as said below
- margin_rows: int32 [512, 8, 512], P('sub'), may hold values from 0 to 1023
Outputs:
- fine_residual: bfloat16 [524288, 128], P('sub')
- coarse_residual: float32 [65536, 128], P('sub')
The draws below stay inside these ranges and needn't reach their ends.
Inputs may be any that keep to these rules, and one draw needn't show every extreme that they name: Symmetric: adjacency[i, s] equals adjacency[(i + o_s) mod 512, s'] with o_s' = -o_s; every subdomain is coupled to both cycle neighbours (slots of offsets 1 and -1); the degrees of subdomains differ widely.
All inputs are finite; a program needn't handle non-finite values.
Results may differ from the reference program's by a relative error of at most 0.0095.
Values may be sent and summed in bfloat16 or wider, within the bound.
No kernel may reach another device: no remote copies, remote signals or barrier semaphores. Data moves between devices by JAX's collectives and lax.ppermute only.
A program may use at most 64 MiB of HBM per device.

```python
import math
import jax
import jax.numpy as jnp
from jax import lax

NLOC = 1024
K = 128
RHS = 128
BLK = 128
TPR = 6
NOFF = 8
OV = 512
NB = 8
NT = 48
SUBS = 512


def draw_adjacency(key, part):
    weights = jax.random.randint(jax.random.fold_in(key, 11), (SUBS,), 0, 5)
    coins = jax.random.randint(jax.random.fold_in(key, 12), (SUBS, 3), 0, 8)
    forward_list = [jnp.ones((SUBS,), jnp.int32)]
    for column, offset in enumerate((2, 4, 8)):
        other = jnp.roll(weights, -offset)
        forward_list.append((coins[:, column] < weights + other).astype(jnp.int32))
    forward = jnp.stack(forward_list, axis=1)
    backward = jnp.stack([jnp.roll(forward[:, column], offset) for column, offset in enumerate((1, 2, 4, 8))], axis=1)
    return jnp.concatenate([forward, backward], axis=1).astype(jnp.int32)


def plant(values, rng, smallest, top_value):
    longest = values.shape.index(max(values.shape))
    spots = []
    for shift in (0, 1):
        where = [jax.random.randint(jax.random.fold_in(rng, axis), (), 0, length) for axis, length in enumerate(values.shape)]
        where[longest] = (where[longest] + shift) % values.shape[longest]
        spots.append(tuple(where))
    return values.at[spots[0]].set(smallest).at[spots[1]].set(top_value)


def block_levels(key, extent, shards, low, largest):
    def one(position, shards_of):
        draws = jax.random.uniform(jax.random.fold_in(jax.random.fold_in(key, 6), position), (shards_of,), jnp.float32, low / len(shards), largest / len(shards))
        return jnp.repeat(jnp.exp(draws), extent[position] // shards_of).reshape((-1,) + (1,) * (len(extent) - position - 1))

    level = one(*shards[0])
    for cut in shards[1:]:
        level = level * one(*cut)
    return level


def scatter_about(own_key, dims, deviation, most, pieces=(), held_as=jnp.bfloat16):
    loudness = block_levels(own_key, dims, pieces, -0.22, 0.18) if pieces else 1.0
    array = jax.random.normal(own_key, dims, jnp.float32) * deviation * loudness
    return jnp.minimum(jnp.maximum(array, -most), most).astype(held_as)


def setup_inputs(seed: int = 0) -> dict:
    keys = jax.random.split(jax.random.key(seed), 8)
    deflation = scatter_about(keys[0], (SUBS * NLOC, K), NLOC ** -0.5, 0.1875, ((0, 512),))
    op_tiles = scatter_about(keys[1], (SUBS * NT, BLK, BLK), (BLK * TPR) ** -0.5, 0.21875, ((0, 512),))
    tile_cols = plant(jax.random.randint(keys[2], (SUBS * NT,), 0, NB), jax.random.fold_in(keys[2], 1), 0, NB - 1).astype(jnp.int32)
    diag_coef = jnp.clip(jnp.exp(math.log(4.0) - 1.3862944 * jax.random.uniform(keys[3], (SUBS * NLOC,), jnp.float32) ** block_levels(keys[3], (SUBS * NLOC,), ((0, 512),), -0.2, 0.2)), 1.0, 4.0)
    fine_rhs = scatter_about(keys[4], (SUBS * NLOC, RHS), 1.0, 6.0, ((0, 512),))
    adjacency = draw_adjacency(jax.random.fold_in(keys[7], 71), 0)
    margin_rows = plant(jax.random.randint(keys[6], (SUBS, NOFF, OV), 0, NLOC), jax.random.fold_in(keys[6], 1), 0, NLOC - 1).astype(jnp.int32)
    return {"deflation": deflation, "op_tiles": op_tiles, "tile_cols": tile_cols, "diag_coef": diag_coef, "fine_rhs": fine_rhs, "adjacency": adjacency, "margin_rows": margin_rows}


OFFSETS = (1, 2, 4, 8, -1, -2, -4, -8)
CHEB_CENTER = 2.5
CHEB_HALF = 1.5
RHO_FIRST = CHEB_HALF / CHEB_CENTER
RHO_SECOND = 1.0 / (2.0 * CHEB_CENTER / CHEB_HALF - RHO_FIRST)


def tile_apply(op_tiles, tile_cols, values_in):
    local_n, columns_n = values_in.shape
    block_n = local_n // BLK
    picked = values_in.reshape(block_n, BLK, columns_n)[tile_cols]
    products = jnp.einsum("tab,tbw->taw", op_tiles.astype(jnp.float32), picked.astype(jnp.float32))
    return products.reshape(block_n, TPR, BLK, columns_n).sum(axis=1).reshape(local_n, columns_n)


def reference(deflation, op_tiles, tile_cols, diag_coef, fine_rhs, adjacency, margin_rows):
    bases = deflation.reshape(SUBS, NLOC, K)
    tiles_all = op_tiles.reshape(SUBS, NT, BLK, BLK)
    columns_all = tile_cols.reshape(SUBS, NT)
    diags = diag_coef.reshape(SUBS, NLOC)
    rights = fine_rhs.reshape(SUBS, NLOC, RHS)
    weights_adj = adjacency.astype(jnp.float32)

    def local_image(packed):
        basis_one, tiles_one, columns_one, diag_one = packed
        result = diag_one[:, None] * basis_one.astype(jnp.float32) + tile_apply(tiles_one, columns_one, basis_one)
        return result.astype(jnp.bfloat16)

    images = lax.map(local_image, (bases, tiles_all, columns_all, diags))

    def blocks(dev_index):
        basis_one = bases[dev_index]
        image_one = images[dev_index]
        own_block = jnp.dot(basis_one.T, image_one, preferred_element_type=jnp.float32)
        rhs_one = jnp.dot(basis_one.T, rights[dev_index], preferred_element_type=jnp.float32)
        pair_list = []
        for slot_id, offset in enumerate(OFFSETS):
            partner = (dev_index + offset) % SUBS
            back_slot = OFFSETS.index(-offset)
            mine_rows = margin_rows[dev_index, slot_id]
            their_rows = margin_rows[partner, back_slot]
            part_basis = bases[partner][their_rows]
            part_image = images[partner][their_rows]
            pair_term = 0.5 * (jnp.dot(basis_one[mine_rows].T, part_image, preferred_element_type=jnp.float32)
                               + jnp.dot(image_one[mine_rows].T, part_basis, preferred_element_type=jnp.float32))
            pair_list.append(pair_term * weights_adj[dev_index, slot_id])
        return own_block, rhs_one, jnp.stack(pair_list)

    own_blocks, coarse_rhs, pair_blocks = lax.map(blocks, jnp.arange(SUBS, dtype=jnp.int32))

    def apply_coarse(vector):
        result = jnp.einsum("skl,slr->skr", own_blocks, vector, precision=lax.Precision.HIGHEST)
        for slot_id, offset in enumerate(OFFSETS):
            remote = jnp.roll(vector, -offset, axis=0)
            result = result + jnp.einsum("skl,slr->skr", pair_blocks[:, slot_id], remote, precision=lax.Precision.HIGHEST)
        return result

    first = coarse_rhs / CHEB_CENTER
    resid_one = coarse_rhs - apply_coarse(first)
    second = RHO_SECOND * RHO_FIRST * first + (2.0 * RHO_SECOND / CHEB_HALF) * resid_one
    coarse_sol = first + second
    coarse_residual = resid_one - apply_coarse(second)
    coeffs = coarse_sol.astype(jnp.bfloat16)

    def correct(packed):
        basis_one, coeff_one = packed
        return jnp.dot(basis_one, coeff_one, preferred_element_type=jnp.float32).astype(jnp.bfloat16)

    local_corr = lax.map(correct, (bases, coeffs))

    def finish(dev_index):
        summed = local_corr[dev_index].astype(jnp.float32)
        for slot_id, offset in enumerate(OFFSETS):
            partner = (dev_index + offset) % SUBS
            back_slot = OFFSETS.index(-offset)
            arrived = local_corr[partner][margin_rows[partner, back_slot]].astype(jnp.float32)
            summed = summed.at[margin_rows[dev_index, slot_id]].add(weights_adj[dev_index, slot_id] * arrived)
        merged = summed.astype(jnp.bfloat16)
        fine_image = diags[dev_index][:, None] * merged.astype(jnp.float32) + tile_apply(tiles_all[dev_index], columns_all[dev_index], merged)
        return (rights[dev_index].astype(jnp.float32) - fine_image).astype(jnp.bfloat16)

    fine_residual = lax.map(finish, jnp.arange(SUBS, dtype=jnp.int32))
    return fine_residual.reshape(SUBS * NLOC, RHS), coarse_residual.reshape(SUBS * K, RHS)
```

```python
import functools

import jax
import jax.numpy as jnp
from jax import lax
from jax.experimental import pallas as pl
from jax.experimental.pallas import tpu as pltpu
from jax.sharding import PartitionSpec as P

BLK = 128
TPR = 6
NB = 8
OV = 512
NLOC = 1024
K = 128
CHEB_CENTER = 2.5
CHEB_HALF = 1.5
RHO_FIRST = CHEB_HALF / CHEB_CENTER
RHO_SECOND = 1.0 / (2.0 * CHEB_CENTER / CHEB_HALF - RHO_FIRST)
F32 = jnp.float32
BF16 = jnp.bfloat16
VMEM = pl.BlockSpec(memory_space=pltpu.VMEM)
SMEM = pl.BlockSpec(memory_space=pltpu.SMEM)
NT = (((1,), (1,)), ((), ()))
STEPS = tuple((power, colour) for power in range(4) for colour in (0, 1))


def swapped(block, power, colour):
    n, o = lax.axis_size("sub"), 1 << power
    route = [(i, (i + o) % n if (i // o) % 2 == colour else (i - o) % n) for i in range(n)]
    return lax.ppermute(block, "sub", route)


def slot_of(step, me):
    power, colour = STEPS[step]
    bit = lax.rem(lax.div(me, 1 << power), 2)
    return power + 4 * (bit if colour == 0 else 1 - bit)


def split(x):
    hi = x.astype(BF16)
    return hi, (x - hi.astype(F32)).astype(BF16)


def column(diag_ref, b):
    return jnp.broadcast_to(diag_ref[b : b + 1, :], (BLK, BLK)).T


def tile_row(cols_ref, tiles_ref, v_ref, b):
    acc = None
    for t in range(TPR * b, TPR * (b + 1)):
        rows = pl.ds(pl.multiple_of(cols_ref[t] * BLK, BLK), BLK)
        term = jnp.dot(tiles_ref[t], v_ref[rows, :], preferred_element_type=F32)
        acc = term if acc is None else acc + term
    return acc


def picks(margin_ref, slot):
    rows = margin_ref[pl.ds(slot, 1), :]
    ids = lax.broadcasted_iota(jnp.int32, (NLOC, OV), 0)
    return jnp.where(ids == rows, 1.0, 0.0).astype(BF16)


def prepare(cols_ref, z_ref, tiles_ref, diag_ref, rhs_ref, margin_ref, *rest):
    payloads, (own_ref, coarse_ref), (zit, im_rhs) = rest[:8], rest[8:10], rest[10:]
    me = lax.axis_index("sub")
    for b in range(NB):
        rows = slice(b * BLK, (b + 1) * BLK)
        z = z_ref[rows, :]
        image = (column(diag_ref, b) * z.astype(F32) + tile_row(cols_ref, tiles_ref, z_ref, b)).astype(BF16)
        zit[:K, rows] = z.T
        zit[K:, rows] = image.T
        im_rhs[rows, :K] = image
        im_rhs[rows, K:] = rhs_ref[rows, :]
    both = jnp.dot(zit[:K, :], im_rhs[...], preferred_element_type=F32)
    own_ref[...] = both[:, :K]
    coarse = both[:, K:]
    coarse_ref[...] = coarse
    hi, lo = split(coarse / CHEB_CENTER)
    for step, out in enumerate(payloads):
        onehot = picks(margin_ref, slot_of(step, me))
        out[:, :OV] = jnp.dot(zit[...], onehot, preferred_element_type=F32).astype(BF16)
        out[:K, OV:] = hi
        out[K:, OV:] = lo


def apply_split(e_hi, e_lo, v_hi, v_lo):
    dot = functools.partial(jnp.dot, preferred_element_type=F32)
    return dot(e_hi, v_hi) + (dot(e_lo, v_hi) + dot(e_hi, v_lo))


def iterate(adj_ref, own_ref, coarse_ref, *rest):
    mine, theirs = rest[:8], rest[8:16]
    ehi_ref, elo_ref, resid_ref, second_ref, send_ref, v_ref = rest[16:]
    me = lax.axis_index("sub")
    coarse = coarse_ref[...]
    first = coarse / CHEB_CENTER
    ehi_ref[:, :K], elo_ref[:, :K] = split(own_ref[...])
    v_ref[:K, :K], v_ref[:K, K:] = split(first)
    for step in range(8):
        block = lax.dot_general(mine[step][:, :OV], theirs[step][:, :OV], NT, preferred_element_type=F32)
        weight = adj_ref[0, slot_of(step, me)].astype(F32) * 0.5
        cols = slice((step + 1) * K, (step + 2) * K)
        ehi_ref[:, cols], elo_ref[:, cols] = split((block[:K, K:] + block[K:, :K]) * weight)
        v_ref[cols, :K] = theirs[step][:K, OV:]
        v_ref[cols, K:] = theirs[step][K:, OV:]
    image = apply_split(ehi_ref[...], elo_ref[...], v_ref[:, :K], v_ref[:, K:])
    resid = coarse - image
    second = RHO_SECOND * RHO_FIRST * first + (2.0 * RHO_SECOND / CHEB_HALF) * resid
    resid_ref[...] = resid
    second_ref[...] = second
    send_ref[:, :K], send_ref[:, K:] = split(second)


def finish(cols_ref, adj_ref, z_ref, tiles_ref, diag_ref, rhs_ref, margin_ref, coarse_ref, ehi_ref, elo_ref, resid_ref, second_ref, *rest):
    theirs, seconds = rest[:8], rest[8:16]
    fine_ref, coarse_out, v_ref, summed, merged = rest[16:]
    me = lax.axis_index("sub")
    second = second_ref[...]
    v_ref[:K, :K], v_ref[:K, K:] = split(second)
    coeffs = (coarse_ref[...] / CHEB_CENTER + second).astype(BF16)
    local = jnp.dot(z_ref[...], coeffs, preferred_element_type=F32)
    summed[...] = local.astype(BF16).astype(F32)
    for step in range(8):
        cols = slice((step + 1) * K, (step + 2) * K)
        arrived_second = seconds[step][...]
        v_ref[cols, :] = arrived_second
        parts = theirs[step][:K, OV:].astype(F32) + theirs[step][K:, OV:].astype(F32)
        parts += arrived_second[:, :K].astype(F32) + arrived_second[:, K:].astype(F32)
        slot = slot_of(step, me)
        corr = jnp.dot(parts.T.astype(BF16), theirs[step][:K, :OV], preferred_element_type=F32).astype(BF16)
        corr = corr * adj_ref[0, slot].astype(BF16)
        summed[...] += lax.dot_general(picks(margin_ref, slot), corr, NT, preferred_element_type=F32)
    coarse_out[...] = resid_ref[...] - apply_split(ehi_ref[...], elo_ref[...], v_ref[:, :K], v_ref[:, K:])
    merged[...] = summed[...].astype(BF16)
    for b in range(NB):
        rows = slice(b * BLK, (b + 1) * BLK)
        image = column(diag_ref, b) * merged[rows, :].astype(F32) + tile_row(cols_ref, tiles_ref, merged, b)
        fine_ref[rows, :] = (rhs_ref[rows, :].astype(F32) - image).astype(BF16)


PARAMS = pltpu.CompilerParams(vmem_limit_bytes=48 * 1024 * 1024)


def arr(shape, dtype):
    return jax.ShapeDtypeStruct(shape, dtype)


def per_device(deflation, op_tiles, tile_cols, diag_coef, fine_rhs, adjacency, margin_rows):
    diag = diag_coef.reshape(NB, BLK)
    margin = margin_rows[0]
    *payloads, own, coarse = pl.pallas_call(
        prepare,
        name="prepare",
        in_specs=[SMEM] + [VMEM] * 5,
        out_specs=[VMEM] * 10,
        out_shape=[arr((2 * K, OV + K), BF16)] * 8 + [arr((K, K), F32)] * 2,
        scratch_shapes=[pltpu.VMEM((2 * K, NLOC), BF16), pltpu.VMEM((NLOC, 2 * K), BF16)],
        compiler_params=PARAMS,
    )(tile_cols, deflation, op_tiles, diag, fine_rhs, margin)
    theirs = [swapped(block, *step) for block, step in zip(payloads, STEPS)]
    ehi, elo, resid, second, send = pl.pallas_call(
        iterate,
        name="iterate",
        in_specs=[SMEM] + [VMEM] * 18,
        out_specs=[VMEM] * 5,
        out_shape=[arr((K, 9 * K), BF16)] * 2 + [arr((K, K), F32)] * 2 + [arr((K, 2 * K), BF16)],
        scratch_shapes=[pltpu.VMEM((9 * K, 2 * K), BF16)],
        compiler_params=PARAMS,
    )(adjacency, own, coarse, *payloads, *theirs)
    seconds = [swapped(send, *step) for step in STEPS]
    return tuple(
        pl.pallas_call(
            finish,
            name="finish",
            in_specs=[SMEM] * 2 + [VMEM] * 26,
            out_specs=[VMEM] * 2,
            out_shape=[arr((NLOC, K), BF16), arr((K, K), F32)],
            scratch_shapes=[
                pltpu.VMEM((9 * K, 2 * K), BF16),
                pltpu.VMEM((NLOC, K), F32),
                pltpu.VMEM((NLOC, K), BF16),
            ],
            compiler_params=PARAMS,
        )(tile_cols, adjacency, deflation, op_tiles, diag, fine_rhs, margin, coarse, ehi, elo, resid, second, *theirs, *seconds)
    )


def solution(mesh):
    return jax.shard_map(
        per_device,
        mesh=mesh,
        in_specs=(P("sub", None), P("sub", None, None), P("sub"), P("sub"), P("sub", None), P("sub", None), P("sub", None, None)),
        out_specs=(P("sub", None), P("sub", None)),
        check_vma=False,
    )
```

```python
import functools

import jax
import jax.numpy as jnp
from jax import lax
from jax.experimental import pallas as pl
from jax.experimental.pallas import tpu as pltpu
from jax.sharding import PartitionSpec as P

BLK = 128
TPR = 6
NB = 8
OV = 512
NLOC = 1024
K = 128
TAIL = K * K // OV
CHEB_CENTER = 2.5
CHEB_HALF = 1.5
RHO_FIRST = CHEB_HALF / CHEB_CENTER
RHO_SECOND = 1.0 / (2.0 * CHEB_CENTER / CHEB_HALF - RHO_FIRST)
F32 = jnp.float32
BF16 = jnp.bfloat16
VMEM = pl.BlockSpec(memory_space=pltpu.VMEM)
SMEM = pl.BlockSpec(memory_space=pltpu.SMEM)
HBM = pl.BlockSpec(memory_space=pltpu.HBM)
NT = (((1,), (1,)), ((), ()))
STEPS = ((2, 0), (2, 1), (1, 0), (1, 1), (0, 1), (3, 0), (3, 1), (0, 0))
INSIDE = STEPS.index((0, 0))
ACROSS = STEPS.index((0, 1))


def permute(block, target):
    n = lax.axis_size("sub")
    return lax.ppermute(block, "sub", [(i, target(i) % n) for i in range(n)])


def swapped(block, power, colour):
    o = 1 << power
    return permute(block, lambda i: i + o if (i // o) % 2 == colour else i - o)


def core_swap(block):
    return permute(block, lambda i: i ^ 1)


def both_ways(block, chips):
    return permute(block, lambda i: i + 2 * chips if i % 2 == 0 else i - 2 * chips)


def bit(me, power):
    return lax.rem(lax.div(me, 1 << power), 2)


def slot_of(step, me):
    power, colour = STEPS[step]
    return power + 4 * (bit(me, power) if colour == 0 else 1 - bit(me, power))


def near_step_is_first(power, me):
    return bit(me, power) != bit(me, 0)


def split(x):
    hi = x.astype(BF16)
    return hi, (x - hi.astype(F32)).astype(BF16)


def column(diag_ref, b):
    return jnp.broadcast_to(diag_ref[b : b + 1, :], (BLK, BLK)).T


def tile_row(cols_ref, tiles_ref, v_ref, b):
    acc = None
    for t in range(TPR * b, TPR * (b + 1)):
        rows = pl.ds(pl.multiple_of(cols_ref[t] * BLK, BLK), BLK)
        term = jnp.dot(tiles_ref[t], v_ref[rows, :], preferred_element_type=F32)
        acc = term if acc is None else acc + term
    return acc


def picks(margin_ref, slot):
    rows = margin_ref[pl.ds(slot, 1), :]
    ids = lax.broadcasted_iota(jnp.int32, (NLOC, OV), 0)
    return jnp.where(ids == rows, 1.0, 0.0).astype(BF16)


def prepare(cols_in, z_in, tiles_in, diag_in, rhs_in, margin_in, *rest):
    payloads, (own_ref, coarse_ref) = rest[:8], rest[8:10]
    cols_ref, z_ref, tiles_ref, diag_ref, rhs_ref, margin_ref, zit, im_rhs, sems = rest[10:]
    me = lax.axis_index("sub")
    pairs = [(cols_in, cols_ref), (z_in, z_ref), (diag_in, diag_ref)]
    pairs += [(tiles_in.at[pl.ds(TPR * b, TPR)], tiles_ref.at[pl.ds(TPR * b, TPR)]) for b in range(NB)]
    pairs += [(rhs_in, rhs_ref), (margin_in, margin_ref)]
    copies = [pltpu.make_async_copy(src, dst, sems.at[i]) for i, (src, dst) in enumerate(pairs)]
    for copy in copies:
        copy.start()
    for copy in copies[:3]:
        copy.wait()
    for b in range(NB):
        copies[3 + b].wait()
        rows = slice(b * BLK, (b + 1) * BLK)
        z = z_ref[rows, :]
        image = (column(diag_ref, b) * z.astype(F32) + tile_row(cols_ref, tiles_ref, z_ref, b)).astype(BF16)
        zit[:K, rows] = z.T
        zit[K:, rows] = image.T
        im_rhs[rows, :K] = image
    copies[-2].wait()
    copies[-1].wait()
    im_rhs[:, K:] = rhs_ref[...]
    both = jnp.dot(zit[:K, :], im_rhs[...], preferred_element_type=F32)
    own_ref[...] = both[:, :K]
    coarse = both[:, K:]
    coarse_ref[...] = coarse
    first = (coarse / CHEB_CENTER).astype(BF16)
    for step, out in enumerate(payloads):
        onehot = picks(margin_ref, slot_of(step, me))
        out[: 2 * K, :] = jnp.dot(zit[...], onehot, preferred_element_type=F32).astype(BF16)
        for q in range(OV // K):
            out[2 * K :, q * K : (q + 1) * K] = first[q * TAIL : (q + 1) * TAIL, :]


dot = functools.partial(jnp.dot, preferred_element_type=F32)


def iterate(adj_ref, own_ref, coarse_ref, *rest):
    mine, theirs = rest[:8], rest[8:16]
    ehi_ref, elo_ref, send_ref, v_ref = rest[16:]
    me = lax.axis_index("sub")
    coarse = coarse_ref[...]
    first = coarse / CHEB_CENTER
    ehi_ref[:, :K], elo_ref[:, :K] = split(own_ref[...])
    v_ref[:K, :], first_lo = split(first)
    for step in range(8):
        block = lax.dot_general(mine[step][: 2 * K, :], theirs[step][: 2 * K, :], NT, preferred_element_type=F32)
        weight = adj_ref[0, slot_of(step, me)].astype(F32) * 0.5
        at = (step + 1) * K
        ehi_ref[:, at : at + K], elo_ref[:, at : at + K] = split((block[:K, K:] + block[K:, :K]) * weight)
        for q in range(OV // K):
            v_ref[at + q * TAIL : at + (q + 1) * TAIL, :] = theirs[step][2 * K :, q * K : (q + 1) * K]
    image = dot(ehi_ref[...], v_ref[...]) + dot(elo_ref[...], v_ref[...]) + dot(ehi_ref[:, :K], first_lo)
    second = RHO_SECOND * RHO_FIRST * first + (2.0 * RHO_SECOND / CHEB_HALF) * (coarse - image)
    send_ref[:, :K], send_ref[:, K:] = split(first + second)


def arrive(adj_ref, margin_ref, slot, basis, coeffs):
    corr = lax.dot_general(coeffs, basis, (((0,), (0,)), ((), ())), preferred_element_type=F32).astype(BF16)
    corr = corr * adj_ref[0, slot].astype(BF16)
    return lax.dot_general(picks(margin_ref, slot), corr, NT, preferred_element_type=F32)


def merge_chip(adj_ref, z_ref, margin_ref, send_ref, other_ref, basis_ref, out_ref):
    me = lax.axis_index("sub")
    local = dot(z_ref[...], send_ref[:, :K]).astype(BF16).astype(F32)
    out_ref[...] = local + arrive(adj_ref, margin_ref, slot_of(INSIDE, me), basis_ref[:K, :], other_ref[:, :K])


def pick_basis(refs, power, near, me):
    a, b = STEPS.index((power, 0)), STEPS.index((power, 1))
    take_a = near_step_is_first(power, me) == near
    slot = jnp.where(take_a, slot_of(a, me), slot_of(b, me))
    return jnp.where(take_a, refs[a][:K, :], refs[b][:K, :]), slot, jnp.where(take_a, a, b)


def merge_near(adj_ref, margin_ref, summed_ref, one_ref, two_ref, four_ref, *rest):
    theirs, out_ref = rest[:8], rest[8]
    me = lax.axis_index("sub")
    acc = summed_ref[...]
    acc += arrive(adj_ref, margin_ref, slot_of(ACROSS, me), theirs[ACROSS][:K, :], one_ref[K:, :K])
    for power, ref in ((1, one_ref), (2, two_ref), (3, four_ref)):
        basis, slot, _ = pick_basis(theirs, power, True, me)
        acc += arrive(adj_ref, margin_ref, slot, basis, ref[:K, :K])
    out_ref[...] = acc


def finish(cols_ref, adj_ref, tiles_ref, diag_ref, rhs_ref, margin_ref, coarse_ref, ehi_ref, elo_ref, summed_ref, send_ref, other_ref, one_ref, two_ref, four_ref, far_ref, *rest):
    theirs = rest[:8]
    fine_ref, coarse_out, v_ref, merged = rest[8:]
    me = lax.axis_index("sub")
    acc = summed_ref[...]
    v_ref[:K, :] = send_ref[...]
    v_ref[(INSIDE + 1) * K : (INSIDE + 2) * K, :] = other_ref[...]
    v_ref[(ACROSS + 1) * K : (ACROSS + 2) * K, :] = one_ref[K:, :]
    for power, ref in ((1, one_ref), (2, two_ref), (3, four_ref)):
        far = far_ref[(power - 1) * K : power * K, :]
        basis, slot, step = pick_basis(theirs, power, False, me)
        acc += arrive(adj_ref, margin_ref, slot, basis, far[:, :K])
        near_step = STEPS.index((power, 0)) + STEPS.index((power, 1)) - step
        v_ref[pl.ds(pl.multiple_of((step + 1) * K, K), K), :] = far
        v_ref[pl.ds(pl.multiple_of((near_step + 1) * K, K), K), :] = ref[:K, :]
    merged[...] = acc.astype(BF16)
    both = dot(ehi_ref[...], v_ref[...])
    coarse_out[...] = coarse_ref[...] - (both[:, :K] + (both[:, K:] + dot(elo_ref[...], v_ref[:, :K])))
    for b in range(NB):
        rows = slice(b * BLK, (b + 1) * BLK)
        image = column(diag_ref, b) * merged[rows, :].astype(F32) + tile_row(cols_ref, tiles_ref, merged, b)
        fine_ref[rows, :] = (rhs_ref[rows, :].astype(F32) - image).astype(BF16)


def arr(shape, dtype):
    return jax.ShapeDtypeStruct(shape, dtype)


def call(kernel, name, in_specs, outs, scratch, flops, limit=32):
    return pl.pallas_call(
        kernel,
        name=name,
        in_specs=in_specs,
        out_specs=[VMEM] * len(outs),
        out_shape=outs,
        scratch_shapes=scratch,
        compiler_params=pltpu.CompilerParams(vmem_limit_bytes=limit * 1024 * 1024),
        cost_estimate=pl.CostEstimate(flops=flops, bytes_accessed=2**20, transcendentals=0),
    )


def per_device(deflation, op_tiles, tile_cols, diag_coef, fine_rhs, adjacency, margin_rows):
    diag = diag_coef.reshape(NB, BLK)
    margin = margin_rows[0]
    *payloads, own, coarse = call(
        prepare,
        "prepare",
        [HBM] * 6,
        [arr((2 * K + TAIL, OV), BF16)] * 8 + [arr((K, K), F32)] * 2,
        [
            pltpu.SMEM((TPR * NB,), jnp.int32),
            pltpu.VMEM((NLOC, K), BF16),
            pltpu.VMEM((TPR * NB, BLK, BLK), BF16),
            pltpu.VMEM((NB, BLK), F32),
            pltpu.VMEM((NLOC, K), BF16),
            pltpu.VMEM((8, OV), jnp.int32),
            pltpu.VMEM((2 * K, NLOC), BF16),
            pltpu.VMEM((NLOC, 2 * K), BF16),
            pltpu.SemaphoreType.DMA((NB + 5,)),
        ],
        3 * 10**9,
    )(*(pltpu.with_memory_space_constraint(x, pltpu.HBM) for x in (tile_cols, deflation, op_tiles, diag, fine_rhs, margin)))
    theirs = [swapped(block, *step) for block, step in zip(payloads, STEPS)]
    ehi, elo, send = call(
        iterate,
        "iterate",
        [SMEM] + [VMEM] * 18,
        [arr((K, 9 * K), BF16)] * 2 + [arr((K, 2 * K), BF16)],
        [pltpu.VMEM((9 * K, K), BF16)],
        10**9,
    )(adjacency, own, coarse, *payloads, *theirs)
    other = core_swap(send)
    pair = jnp.concatenate([send, other])
    one, two, four = (both_ways(pair, chips) for chips in (1, 2, 4))
    summed = call(
        merge_chip, "merge_chip", [SMEM] + [VMEM] * 5, [arr((NLOC, K), F32)], [], 10**9
    )(adjacency, deflation, margin, send, other, theirs[INSIDE])[0]
    hand_over, summed = lax.optimization_barrier((jnp.concatenate([one[K:], two[K:], four[K:]]), summed))
    far = core_swap(hand_over)
    summed = call(
        merge_near, "merge_near", [SMEM] + [VMEM] * 13, [arr((NLOC, K), F32)], [], 2 * 10**9
    )(adjacency, margin, summed, one, two, four, *theirs)[0]
    return tuple(
        call(
            finish,
            "finish",
            [SMEM] * 2 + [VMEM] * 22,
            [arr((NLOC, K), BF16), arr((K, K), F32)],
            [pltpu.VMEM((9 * K, 2 * K), BF16), pltpu.VMEM((NLOC, K), BF16)],
            3 * 10**9,
        )(tile_cols, adjacency, op_tiles, diag, fine_rhs, margin, coarse, ehi, elo, summed, send, other, one, two, four, far, *theirs)
    )


def solution(mesh):
    return jax.shard_map(
        per_device,
        mesh=mesh,
        in_specs=(P("sub", None), P("sub", None, None), P("sub"), P("sub"), P("sub", None), P("sub", None), P("sub", None, None)),
        out_specs=(P("sub", None), P("sub", None)),
        check_vma=False,
    )
```

```python
import functools

import jax
import jax.numpy as jnp
from jax import lax
from jax.experimental import pallas as pl
from jax.experimental.pallas import tpu as pltpu
from jax.sharding import PartitionSpec as P

BLK = 128
TPR = 6
NB = 8
OV = 512
NLOC = 1024
K = 128
TAIL = K * K // OV
CHEB_CENTER = 2.5
CHEB_HALF = 1.5
RHO_FIRST = CHEB_HALF / CHEB_CENTER
RHO_SECOND = 1.0 / (2.0 * CHEB_CENTER / CHEB_HALF - RHO_FIRST)
F32 = jnp.float32
BF16 = jnp.bfloat16
VMEM = pl.BlockSpec(memory_space=pltpu.VMEM)
SMEM = pl.BlockSpec(memory_space=pltpu.SMEM)
HBM = pl.BlockSpec(memory_space=pltpu.HBM)
NT = (((1,), (1,)), ((), ()))
STEPS = ((0, 0), (2, 0), (2, 1), (3, 0), (1, 0), (1, 1), (3, 1), (0, 1))
EARLY = 6
INSIDE = STEPS.index((0, 0))
ACROSS = STEPS.index((0, 1))


def permute(block, target):
    n = lax.axis_size("sub")
    return lax.ppermute(block, "sub", [(i, target(i) % n) for i in range(n)])


def swapped(block, power, colour):
    o = 1 << power
    return permute(block, lambda i: i + o if (i // o) % 2 == colour else i - o)


def core_swap(block):
    return permute(block, lambda i: i ^ 1)


def both_ways(block, chips):
    return permute(block, lambda i: i + 2 * chips if i % 2 == 0 else i - 2 * chips)


def bit(me, power):
    return lax.rem(lax.div(me, 1 << power), 2)


def slot_of(step, me):
    power, colour = STEPS[step]
    return power + 4 * (bit(me, power) if colour == 0 else 1 - bit(me, power))


def near_step_is_first(power, me):
    return bit(me, power) != bit(me, 0)


def split(x):
    hi = x.astype(BF16)
    return hi, (x - hi.astype(F32)).astype(BF16)


def column(diag_ref, b):
    return jnp.broadcast_to(diag_ref[b : b + 1, :], (BLK, BLK)).T


def tile_row(cols_ref, tiles_ref, v_ref, b):
    acc = None
    for t in range(TPR * b, TPR * (b + 1)):
        rows = pl.ds(pl.multiple_of(cols_ref[t] * BLK, BLK), BLK)
        term = jnp.dot(tiles_ref[t], v_ref[rows, :], preferred_element_type=F32)
        acc = term if acc is None else acc + term
    return acc


def picks(margin_ref, slot):
    rows = margin_ref[pl.ds(slot, 1), :]
    ids = lax.broadcasted_iota(jnp.int32, (NLOC, OV), 0)
    return jnp.where(ids == rows, 1.0, 0.0).astype(BF16)


def prepare(cols_in, z_in, tiles_in, diag_in, rhs_in, margin_in, *rest):
    payloads, (own_ref, coarse_ref) = rest[:8], rest[8:10]
    cols_ref, z_ref, tiles_ref, diag_ref, rhs_ref, margin_ref, zit, im_rhs, sems = rest[10:]
    me = lax.axis_index("sub")
    pairs = [(cols_in, cols_ref), (z_in, z_ref), (diag_in, diag_ref)]
    pairs += [(tiles_in.at[pl.ds(TPR * b, TPR)], tiles_ref.at[pl.ds(TPR * b, TPR)]) for b in range(NB)]
    pairs += [(rhs_in, rhs_ref), (margin_in, margin_ref)]
    copies = [pltpu.make_async_copy(src, dst, sems.at[i]) for i, (src, dst) in enumerate(pairs)]
    for copy in copies:
        copy.start()
    for copy in copies[:3]:
        copy.wait()
    for b in range(NB):
        copies[3 + b].wait()
        rows = slice(b * BLK, (b + 1) * BLK)
        z = z_ref[rows, :]
        image = (column(diag_ref, b) * z.astype(F32) + tile_row(cols_ref, tiles_ref, z_ref, b)).astype(BF16)
        zit[:K, rows] = z.T
        zit[K:, rows] = image.T
        im_rhs[rows, :K] = image
    copies[-2].wait()
    copies[-1].wait()
    im_rhs[:, K:] = rhs_ref[...]
    both = jnp.dot(zit[:K, :], im_rhs[...], preferred_element_type=F32)
    own_ref[...] = both[:, :K]
    coarse = both[:, K:]
    coarse_ref[...] = coarse
    first = (coarse / CHEB_CENTER).astype(BF16)
    for step, out in enumerate(payloads):
        onehot = picks(margin_ref, slot_of(step, me))
        out[: 2 * K, :] = jnp.dot(zit[...], onehot, preferred_element_type=F32).astype(BF16)
        for q in range(OV // K):
            out[2 * K :, q * K : (q + 1) * K] = first[q * TAIL : (q + 1) * TAIL, :]


dot = functools.partial(jnp.dot, preferred_element_type=F32)


def pair_block(mine, theirs, adj_ref, step, me):
    block = lax.dot_general(mine[: 2 * K, :], theirs[: 2 * K, :], NT, preferred_element_type=F32)
    weight = adj_ref[0, slot_of(step, me)].astype(F32) * 0.5
    return split((block[:K, K:] + block[K:, :K]) * weight)


def take_first(theirs, v_ref, at):
    for q in range(OV // K):
        v_ref[at + q * TAIL : at + (q + 1) * TAIL, :] = theirs[2 * K :, q * K : (q + 1) * K]


def iterate_early(adj_ref, own_ref, coarse_ref, *rest):
    mine, theirs = rest[:EARLY], rest[EARLY : 2 * EARLY]
    ehi_ref, elo_ref, image_ref, v_ref = rest[2 * EARLY :]
    me = lax.axis_index("sub")
    ehi_ref[:, :K], elo_ref[:, :K] = split(own_ref[...])
    v_ref[:K, :], first_lo = split(coarse_ref[...] / CHEB_CENTER)
    for step in range(EARLY):
        at = (step + 1) * K
        ehi_ref[:, at : at + K], elo_ref[:, at : at + K] = pair_block(mine[step], theirs[step], adj_ref, step, me)
        take_first(theirs[step], v_ref, at)
    image_ref[...] = dot(ehi_ref[...], v_ref[...]) + dot(elo_ref[...], v_ref[...]) + dot(ehi_ref[:, :K], first_lo)


def iterate(adj_ref, coarse_ref, image_ref, *rest):
    late = 8 - EARLY
    mine, theirs = rest[:late], rest[late : 2 * late]
    ehi_ref, elo_ref, send_ref, v_ref = rest[2 * late :]
    me = lax.axis_index("sub")
    coarse = coarse_ref[...]
    first = coarse / CHEB_CENTER
    for i in range(late):
        at = i * K
        ehi_ref[:, at : at + K], elo_ref[:, at : at + K] = pair_block(mine[i], theirs[i], adj_ref, EARLY + i, me)
        take_first(theirs[i], v_ref, at)
    image = image_ref[...] + (dot(ehi_ref[...], v_ref[...]) + dot(elo_ref[...], v_ref[...]))
    second = RHO_SECOND * RHO_FIRST * first + (2.0 * RHO_SECOND / CHEB_HALF) * (coarse - image)
    send_ref[:, :K], send_ref[:, K:] = split(first + second)


def arrive(adj_ref, margin_ref, slot, basis, coeffs):
    corr = lax.dot_general(coeffs, basis, (((0,), (0,)), ((), ())), preferred_element_type=F32).astype(BF16)
    corr = corr * adj_ref[0, slot].astype(BF16)
    return lax.dot_general(picks(margin_ref, slot), corr, NT, preferred_element_type=F32)


def merge_chip(adj_ref, z_ref, margin_ref, send_ref, other_ref, basis_ref, out_ref):
    me = lax.axis_index("sub")
    local = dot(z_ref[...], send_ref[:, :K]).astype(BF16).astype(F32)
    out_ref[...] = local + arrive(adj_ref, margin_ref, slot_of(INSIDE, me), basis_ref[:K, :], other_ref[:, :K])


def pick_basis(power, a_ref, b_ref, near, me):
    a, b = STEPS.index((power, 0)), STEPS.index((power, 1))
    take_a = near_step_is_first(power, me) == near
    slot = jnp.where(take_a, slot_of(a, me), slot_of(b, me))
    return jnp.where(take_a, a_ref[:K, :], b_ref[:K, :]), slot, jnp.where(take_a, a, b)


def merge_near(power, adj_ref, margin_ref, summed_ref, vectors_ref, a_ref, b_ref, out_ref):
    me = lax.axis_index("sub")
    basis, slot, _ = pick_basis(power, a_ref, b_ref, True, me)
    out_ref[...] = summed_ref[...] + arrive(adj_ref, margin_ref, slot, basis, vectors_ref[:K, :K])


def merge_next(adj_ref, margin_ref, summed_ref, vectors_ref, across_ref, a_ref, b_ref, out_ref):
    me = lax.axis_index("sub")
    acc = summed_ref[...] + arrive(adj_ref, margin_ref, slot_of(ACROSS, me), across_ref[:K, :], vectors_ref[K:, :K])
    basis, slot, _ = pick_basis(1, a_ref, b_ref, True, me)
    out_ref[...] = acc + arrive(adj_ref, margin_ref, slot, basis, vectors_ref[:K, :K])


def finish(cols_ref, adj_ref, tiles_ref, diag_ref, rhs_ref, margin_ref, coarse_ref, ehi_early, elo_early, ehi_late, elo_late, summed_ref, send_ref, other_ref, one_ref, two_ref, four_ref, far_ref, *rest):
    theirs = rest[:8]
    fine_ref, coarse_out, v_ref, merged = rest[8:]
    me = lax.axis_index("sub")
    acc = summed_ref[...]
    v_ref[:K, :] = send_ref[...]
    v_ref[(INSIDE + 1) * K : (INSIDE + 2) * K, :] = other_ref[...]
    v_ref[(ACROSS + 1) * K : (ACROSS + 2) * K, :] = one_ref[K:, :]
    for power, ref in ((1, one_ref), (2, two_ref), (3, four_ref)):
        far = far_ref[(power - 1) * K : power * K, :]
        a, b = STEPS.index((power, 0)), STEPS.index((power, 1))
        basis, slot, step = pick_basis(power, theirs[a], theirs[b], False, me)
        acc += arrive(adj_ref, margin_ref, slot, basis, far[:, :K])
        near_step = a + b - step
        v_ref[pl.ds(pl.multiple_of((step + 1) * K, K), K), :] = far
        v_ref[pl.ds(pl.multiple_of((near_step + 1) * K, K), K), :] = ref[:K, :]
    merged[...] = acc.astype(BF16)
    early, late = slice(0, (EARLY + 1) * K), slice((EARLY + 1) * K, 9 * K)
    both = dot(ehi_early[...], v_ref[early, :]) + dot(ehi_late[...], v_ref[late, :])
    small = dot(elo_early[...], v_ref[early, :K]) + dot(elo_late[...], v_ref[late, :K])
    coarse_out[...] = coarse_ref[...] - (both[:, :K] + (both[:, K:] + small))
    for b in range(NB):
        rows = slice(b * BLK, (b + 1) * BLK)
        image = column(diag_ref, b) * merged[rows, :].astype(F32) + tile_row(cols_ref, tiles_ref, merged, b)
        fine_ref[rows, :] = (rhs_ref[rows, :].astype(F32) - image).astype(BF16)


def arr(shape, dtype):
    return jax.ShapeDtypeStruct(shape, dtype)


def call(kernel, name, in_specs, outs, scratch, flops, limit=32, moved=2**20):
    return pl.pallas_call(
        kernel,
        name=name,
        in_specs=in_specs,
        out_specs=[VMEM] * len(outs),
        out_shape=outs,
        scratch_shapes=scratch,
        compiler_params=pltpu.CompilerParams(vmem_limit_bytes=limit * 1024 * 1024),
        cost_estimate=pl.CostEstimate(flops=flops, bytes_accessed=moved, transcendentals=0),
    )


def per_device(deflation, op_tiles, tile_cols, diag_coef, fine_rhs, adjacency, margin_rows):
    diag = diag_coef.reshape(NB, BLK)
    margin = margin_rows[0]
    *payloads, own, coarse = call(
        prepare,
        "prepare",
        [HBM] * 6,
        [arr((2 * K + TAIL, OV), BF16)] * 8 + [arr((K, K), F32)] * 2,
        [
            pltpu.SMEM((TPR * NB,), jnp.int32),
            pltpu.VMEM((NLOC, K), BF16),
            pltpu.VMEM((TPR * NB, BLK, BLK), BF16),
            pltpu.VMEM((NB, BLK), F32),
            pltpu.VMEM((NLOC, K), BF16),
            pltpu.VMEM((8, OV), jnp.int32),
            pltpu.VMEM((2 * K, NLOC), BF16),
            pltpu.VMEM((NLOC, 2 * K), BF16),
            pltpu.SemaphoreType.DMA((NB + 5,)),
        ],
        3 * 10**9,
    )(*(pltpu.with_memory_space_constraint(x, pltpu.HBM) for x in (tile_cols, deflation, op_tiles, diag, fine_rhs, margin)))
    theirs = [swapped(block, *step) for block, step in zip(payloads, STEPS)]
    early = (EARLY + 1) * K
    ehi_early, elo_early, image = call(
        iterate_early,
        "iterate_early",
        [SMEM] + [VMEM] * (2 + 2 * EARLY),
        [arr((K, early), BF16)] * 2 + [arr((K, K), F32)],
        [pltpu.VMEM((early, K), BF16)],
        10**9,
    )(adjacency, own, coarse, *payloads[:EARLY], *theirs[:EARLY])
    late = (8 - EARLY) * K
    ehi_late, elo_late, send = call(
        iterate,
        "iterate",
        [SMEM] + [VMEM] * (2 + 2 * (8 - EARLY)),
        [arr((K, late), BF16)] * 2 + [arr((K, 2 * K), BF16)],
        [pltpu.VMEM((late, K), BF16)],
        10**9,
    )(adjacency, coarse, image, *payloads[EARLY:], *theirs[EARLY:])
    other = core_swap(send)
    pair = jnp.concatenate([send, other])
    one, two, four = (both_ways(pair, chips) for chips in (1, 2, 4))
    summed = call(
        merge_chip, "merge_chip", [SMEM] + [VMEM] * 5, [arr((NLOC, K), F32)], [], 10**9
    )(adjacency, deflation, margin, send, other, theirs[INSIDE])[0]
    near = {power: [theirs[STEPS.index((power, colour))] for colour in (0, 1)] for power in (1, 2, 3)}
    for power, vectors in ((3, four), (2, two)):
        summed = call(
            functools.partial(merge_near, power), f"merge_{power}", [SMEM] + [VMEM] * 5, [arr((NLOC, K), F32)], [], 1, moved=1
        )(adjacency, margin, summed, vectors, *near[power])[0]
    one_late, summed = lax.optimization_barrier((one, summed))
    hand_over = jnp.concatenate([one_late[K:], two[K:], four[K:]])
    far = core_swap(hand_over)
    summed = call(merge_next, "merge_next", [SMEM] + [VMEM] * 6, [arr((NLOC, K), F32)], [], 10**9)(
        adjacency, margin, summed, one, theirs[ACROSS], *near[1]
    )[0]
    return tuple(
        call(
            finish,
            "finish",
            [SMEM] * 2 + [VMEM] * 24,
            [arr((NLOC, K), BF16), arr((K, K), F32)],
            [pltpu.VMEM((9 * K, 2 * K), BF16), pltpu.VMEM((NLOC, K), BF16)],
            3 * 10**9,
        )(tile_cols, adjacency, op_tiles, diag, fine_rhs, margin, coarse, ehi_early, elo_early, ehi_late, elo_late, summed, send, other, one, two, four, far, *theirs)
    )


def solution(mesh):
    return jax.shard_map(
        per_device,
        mesh=mesh,
        in_specs=(P("sub", None), P("sub", None, None), P("sub"), P("sub"), P("sub", None), P("sub", None), P("sub", None, None)),
        out_specs=(P("sub", None), P("sub", None)),
        check_vma=False,
    )
```

```python
import functools

import jax
import jax.numpy as jnp
from jax import lax
from jax.experimental import pallas as pl
from jax.experimental.pallas import tpu as pltpu
from jax.sharding import PartitionSpec as P

BLK = 128
TPR = 6
NB = 8
OV = 512
NLOC = 1024
K = 128
TAIL = K * K // OV
CHEB_CENTER = 2.5
CHEB_HALF = 1.5
RHO_FIRST = CHEB_HALF / CHEB_CENTER
RHO_SECOND = 1.0 / (2.0 * CHEB_CENTER / CHEB_HALF - RHO_FIRST)
F32 = jnp.float32
BF16 = jnp.bfloat16
VMEM = pl.BlockSpec(memory_space=pltpu.VMEM)
SMEM = pl.BlockSpec(memory_space=pltpu.SMEM)
HBM = pl.BlockSpec(memory_space=pltpu.HBM)
NT = (((1,), (1,)), ((), ()))
STEPS = ((2, 0), (2, 1), (1, 0), (1, 1), (0, 1), (3, 0), (3, 1), (0, 0))
EARLY = 6
INSIDE = STEPS.index((0, 0))
ACROSS = STEPS.index((0, 1))


def permute(block, target):
    n = lax.axis_size("sub")
    return lax.ppermute(block, "sub", [(i, target(i) % n) for i in range(n)])


def swapped(block, power, colour):
    o = 1 << power
    return permute(block, lambda i: i + o if (i // o) % 2 == colour else i - o)


def core_swap(block):
    return permute(block, lambda i: i ^ 1)


def both_ways(block, chips):
    return permute(block, lambda i: i + 2 * chips if i % 2 == 0 else i - 2 * chips)


def bit(me, power):
    return lax.rem(lax.div(me, 1 << power), 2)


def slot_of(step, me):
    power, colour = STEPS[step]
    return power + 4 * (bit(me, power) if colour == 0 else 1 - bit(me, power))


def near_step_is_first(power, me):
    return bit(me, power) != bit(me, 0)


def split(x):
    hi = x.astype(BF16)
    return hi, (x - hi.astype(F32)).astype(BF16)


def column(diag_ref, b):
    return jnp.broadcast_to(diag_ref[b : b + 1, :], (BLK, BLK)).T


def tile_row(cols_ref, tiles_ref, v_ref, b):
    acc = None
    for t in range(TPR * b, TPR * (b + 1)):
        rows = pl.ds(pl.multiple_of(cols_ref[t] * BLK, BLK), BLK)
        term = jnp.dot(tiles_ref[t], v_ref[rows, :], preferred_element_type=F32)
        acc = term if acc is None else acc + term
    return acc


def picks(margin_ref, slot):
    rows = margin_ref[pl.ds(slot, 1), :]
    ids = lax.broadcasted_iota(jnp.int32, (NLOC, OV), 0)
    return jnp.where(ids == rows, 1.0, 0.0).astype(BF16)


def prepare(cols_in, z_in, tiles_in, diag_in, rhs_in, margin_in, *rest):
    payloads, (own_ref, coarse_ref) = rest[:8], rest[8:10]
    cols_ref, z_ref, tiles_ref, diag_ref, rhs_ref, margin_ref, zit, images, sems = rest[10:]
    me = lax.axis_index("sub")
    pairs = [(z_in, z_ref), (rhs_in, rhs_ref), (cols_in, cols_ref), (diag_in, diag_ref)]
    pairs += [(tiles_in.at[pl.ds(TPR * b, TPR)], tiles_ref.at[pl.ds(TPR * b, TPR)]) for b in range(NB)]
    pairs += [(margin_in, margin_ref)]
    copies = [pltpu.make_async_copy(src, dst, sems.at[i]) for i, (src, dst) in enumerate(pairs)]
    for copy in copies:
        copy.start()
    copies[0].wait()
    for b in range(NB):
        rows = slice(b * BLK, (b + 1) * BLK)
        zit[:K, rows] = z_ref[rows, :].T
    for copy in copies[1:4]:
        copy.wait()
    coarse = jnp.dot(zit[:K, :], rhs_ref[...], preferred_element_type=F32)
    coarse_ref[...] = coarse
    first = (coarse / CHEB_CENTER).astype(BF16)
    for copy in copies[4:]:
        copy.wait()
    for b in range(NB):
        rows = slice(b * BLK, (b + 1) * BLK)
        z = z_ref[rows, :]
        image = (column(diag_ref, b) * z.astype(F32) + tile_row(cols_ref, tiles_ref, z_ref, b)).astype(BF16)
        zit[K:, rows] = image.T
        images[rows, :] = image
    for step, out in enumerate(payloads):
        onehot = picks(margin_ref, slot_of(step, me))
        out[: 2 * K, :] = jnp.dot(zit[...], onehot, preferred_element_type=F32).astype(BF16)
        for q in range(OV // K):
            out[2 * K :, q * K : (q + 1) * K] = first[q * TAIL : (q + 1) * TAIL, :]
    own_ref[...] = jnp.dot(zit[:K, :], images[...], preferred_element_type=F32)


dot = functools.partial(jnp.dot, preferred_element_type=F32)


def pair_block(mine, theirs, adj_ref, step, me):
    block = lax.dot_general(mine[: 2 * K, :], theirs[: 2 * K, :], NT, preferred_element_type=F32)
    weight = adj_ref[0, slot_of(step, me)].astype(F32) * 0.5
    return split((block[:K, K:] + block[K:, :K]) * weight)


def take_first(theirs, v_ref, at):
    for q in range(OV // K):
        v_ref[at + q * TAIL : at + (q + 1) * TAIL, :] = theirs[2 * K :, q * K : (q + 1) * K]


def iterate_early(adj_ref, own_ref, coarse_ref, *rest):
    mine, theirs = rest[:EARLY], rest[EARLY : 2 * EARLY]
    ehi_ref, elo_ref, image_ref, v_ref = rest[2 * EARLY :]
    me = lax.axis_index("sub")
    ehi_ref[:, :K], elo_ref[:, :K] = split(own_ref[...])
    v_ref[:K, :], first_lo = split(coarse_ref[...] / CHEB_CENTER)
    for step in range(EARLY):
        at = (step + 1) * K
        ehi_ref[:, at : at + K], elo_ref[:, at : at + K] = pair_block(mine[step], theirs[step], adj_ref, step, me)
        take_first(theirs[step], v_ref, at)
    image_ref[...] = dot(ehi_ref[...], v_ref[...]) + dot(elo_ref[...], v_ref[...]) + dot(ehi_ref[:, :K], first_lo)


def iterate(adj_ref, coarse_ref, image_ref, *rest):
    late = 8 - EARLY
    mine, theirs = rest[:late], rest[late : 2 * late]
    ehi_ref, elo_ref, send_ref, v_ref = rest[2 * late :]
    me = lax.axis_index("sub")
    coarse = coarse_ref[...]
    first = coarse / CHEB_CENTER
    for i in range(late):
        at = i * K
        ehi_ref[:, at : at + K], elo_ref[:, at : at + K] = pair_block(mine[i], theirs[i], adj_ref, EARLY + i, me)
        take_first(theirs[i], v_ref, at)
    image = image_ref[...] + (dot(ehi_ref[...], v_ref[...]) + dot(elo_ref[...], v_ref[...]))
    second = RHO_SECOND * RHO_FIRST * first + (2.0 * RHO_SECOND / CHEB_HALF) * (coarse - image)
    send_ref[:, :K], send_ref[:, K:] = split(first + second)


def arrive(adj_ref, margin_ref, slot, basis, coeffs):
    corr = lax.dot_general(coeffs, basis, (((0,), (0,)), ((), ())), preferred_element_type=F32).astype(BF16)
    corr = corr * adj_ref[0, slot].astype(BF16)
    return lax.dot_general(picks(margin_ref, slot), corr, NT, preferred_element_type=F32)


def corrections(adj_ref, pieces):
    out = []
    for slot, basis, coeffs in pieces:
        corr = lax.dot_general(coeffs, basis, (((0,), (0,)), ((), ())), preferred_element_type=F32).astype(BF16)
        out.append(corr * adj_ref[0, slot].astype(BF16))
    return out


def scatter(margin_ref, slots, corrs):
    onehot = jnp.concatenate([picks(margin_ref, slot) for slot in slots], axis=1)
    return lax.dot_general(onehot, jnp.concatenate(corrs, axis=1), NT, preferred_element_type=F32)


def merge_chip(adj_ref, z_ref, margin_ref, send_ref, other_ref, basis_ref, out_ref):
    me = lax.axis_index("sub")
    local = dot(z_ref[...], send_ref[:, :K]).astype(BF16).astype(F32)
    out_ref[...] = local + arrive(adj_ref, margin_ref, slot_of(INSIDE, me), basis_ref[:K, :], other_ref[:, :K])


def pick_basis(power, a_ref, b_ref, near, me):
    a, b = STEPS.index((power, 0)), STEPS.index((power, 1))
    take_a = near_step_is_first(power, me) == near
    slot = jnp.where(take_a, slot_of(a, me), slot_of(b, me))
    return jnp.where(take_a, a_ref[:K, :], b_ref[:K, :]), slot, jnp.where(take_a, a, b)


def merge_near(power, adj_ref, margin_ref, summed_ref, vectors_ref, a_ref, b_ref, out_ref):
    me = lax.axis_index("sub")
    basis, slot, _ = pick_basis(power, a_ref, b_ref, True, me)
    out_ref[...] = summed_ref[...] + arrive(adj_ref, margin_ref, slot, basis, vectors_ref[:K, :K])


def merge_next(adj_ref, margin_ref, summed_ref, vectors_ref, across_ref, a_ref, b_ref, out_ref):
    me = lax.axis_index("sub")
    basis, slot, _ = pick_basis(1, a_ref, b_ref, True, me)
    slots = (slot_of(ACROSS, me), slot)
    corrs = corrections(adj_ref, ((slots[0], across_ref[:K, :], vectors_ref[K:, :K]), (slot, basis, vectors_ref[:K, :K])))
    out_ref[...] = summed_ref[...] + scatter(margin_ref, slots, corrs)


def finish(cols_ref, adj_ref, tiles_ref, diag_ref, rhs_ref, margin_ref, coarse_ref, ehi_early, elo_early, ehi_late, elo_late, summed_ref, send_ref, other_ref, one_ref, two_ref, four_ref, far_ref, *rest):
    theirs = rest[:8]
    fine_ref, coarse_out, v_ref, merged = rest[8:]
    me = lax.axis_index("sub")
    pieces = []
    v_ref[:K, :] = send_ref[...]
    v_ref[(INSIDE + 1) * K : (INSIDE + 2) * K, :] = other_ref[...]
    v_ref[(ACROSS + 1) * K : (ACROSS + 2) * K, :] = one_ref[K:, :]
    for power, ref in ((1, one_ref), (2, two_ref), (3, four_ref)):
        far = far_ref[(power - 1) * K : power * K, :]
        a, b = STEPS.index((power, 0)), STEPS.index((power, 1))
        basis, slot, step = pick_basis(power, theirs[a], theirs[b], False, me)
        pieces.append((slot, basis, far[:, :K]))
        near_step = a + b - step
        v_ref[pl.ds(pl.multiple_of((step + 1) * K, K), K), :] = far
        v_ref[pl.ds(pl.multiple_of((near_step + 1) * K, K), K), :] = ref[:K, :]
    added = scatter(margin_ref, [p[0] for p in pieces], corrections(adj_ref, pieces))
    merged[...] = (summed_ref[...] + added).astype(BF16)
    early, late = slice(0, (EARLY + 1) * K), slice((EARLY + 1) * K, 9 * K)
    both = dot(ehi_early[...], v_ref[early, :]) + dot(ehi_late[...], v_ref[late, :])
    small = dot(elo_early[...], v_ref[early, :K]) + dot(elo_late[...], v_ref[late, :K])
    coarse_out[...] = coarse_ref[...] - (both[:, :K] + (both[:, K:] + small))
    for b in range(NB):
        rows = slice(b * BLK, (b + 1) * BLK)
        image = column(diag_ref, b) * merged[rows, :].astype(F32) + tile_row(cols_ref, tiles_ref, merged, b)
        fine_ref[rows, :] = (rhs_ref[rows, :].astype(F32) - image).astype(BF16)


def arr(shape, dtype):
    return jax.ShapeDtypeStruct(shape, dtype)


def call(kernel, name, in_specs, outs, scratch, flops, limit=32, moved=2**20):
    return pl.pallas_call(
        kernel,
        name=name,
        in_specs=in_specs,
        out_specs=[VMEM] * len(outs),
        out_shape=outs,
        scratch_shapes=scratch,
        compiler_params=pltpu.CompilerParams(vmem_limit_bytes=limit * 1024 * 1024),
        cost_estimate=pl.CostEstimate(flops=flops, bytes_accessed=moved, transcendentals=0),
    )


def per_device(deflation, op_tiles, tile_cols, diag_coef, fine_rhs, adjacency, margin_rows):
    diag = diag_coef.reshape(NB, BLK)
    margin = margin_rows[0]
    *payloads, own, coarse = call(
        prepare,
        "prepare",
        [HBM] * 6,
        [arr((2 * K + TAIL, OV), BF16)] * 8 + [arr((K, K), F32)] * 2,
        [
            pltpu.SMEM((TPR * NB,), jnp.int32),
            pltpu.VMEM((NLOC, K), BF16),
            pltpu.VMEM((TPR * NB, BLK, BLK), BF16),
            pltpu.VMEM((NB, BLK), F32),
            pltpu.VMEM((NLOC, K), BF16),
            pltpu.VMEM((8, OV), jnp.int32),
            pltpu.VMEM((2 * K, NLOC), BF16),
            pltpu.VMEM((NLOC, K), BF16),
            pltpu.SemaphoreType.DMA((NB + 5,)),
        ],
        3 * 10**9,
    )(*(pltpu.with_memory_space_constraint(x, pltpu.HBM) for x in (tile_cols, deflation, op_tiles, diag, fine_rhs, margin)))
    theirs = [swapped(block, *step) for block, step in zip(payloads, STEPS)]
    early = (EARLY + 1) * K
    ehi_early, elo_early, image = call(
        iterate_early,
        "iterate_early",
        [SMEM] + [VMEM] * (2 + 2 * EARLY),
        [arr((K, early), BF16)] * 2 + [arr((K, K), F32)],
        [pltpu.VMEM((early, K), BF16)],
        10**9,
    )(adjacency, own, coarse, *payloads[:EARLY], *theirs[:EARLY])
    late = (8 - EARLY) * K
    ehi_late, elo_late, send = call(
        iterate,
        "iterate",
        [SMEM] + [VMEM] * (2 + 2 * (8 - EARLY)),
        [arr((K, late), BF16)] * 2 + [arr((K, 2 * K), BF16)],
        [pltpu.VMEM((late, K), BF16)],
        10**9,
    )(adjacency, coarse, image, *payloads[EARLY:], *theirs[EARLY:])
    other = core_swap(send)
    pair = jnp.concatenate([send, other])
    one, two, four = (both_ways(pair, chips) for chips in (1, 2, 4))
    summed = call(
        merge_chip, "merge_chip", [SMEM] + [VMEM] * 5, [arr((NLOC, K), F32)], [], 10**9
    )(adjacency, deflation, margin, send, other, theirs[INSIDE])[0]
    near = {power: [theirs[STEPS.index((power, colour))] for colour in (0, 1)] for power in (1, 2, 3)}
    for power, vectors in ((3, four), (2, two)):
        summed = call(
            functools.partial(merge_near, power), f"merge_{power}", [SMEM] + [VMEM] * 5, [arr((NLOC, K), F32)], [], 1, moved=1
        )(adjacency, margin, summed, vectors, *near[power])[0]
    one_late, summed = lax.optimization_barrier((one, summed))
    hand_over = jnp.concatenate([one_late[K:], two[K:], four[K:]])
    far = core_swap(hand_over)
    summed = call(merge_next, "merge_next", [SMEM] + [VMEM] * 6, [arr((NLOC, K), F32)], [], 10**9)(
        adjacency, margin, summed, one, theirs[ACROSS], *near[1]
    )[0]
    return tuple(
        call(
            finish,
            "finish",
            [SMEM] * 2 + [VMEM] * 24,
            [arr((NLOC, K), BF16), arr((K, K), F32)],
            [pltpu.VMEM((9 * K, 2 * K), BF16), pltpu.VMEM((NLOC, K), BF16)],
            3 * 10**9,
        )(tile_cols, adjacency, op_tiles, diag, fine_rhs, margin, coarse, ehi_early, elo_early, ehi_late, elo_late, summed, send, other, one, two, four, far, *theirs)
    )


def solution(mesh):
    return jax.shard_map(
        per_device,
        mesh=mesh,
        in_specs=(P("sub", None), P("sub", None, None), P("sub"), P("sub"), P("sub", None), P("sub", None), P("sub", None, None)),
        out_specs=(P("sub", None), P("sub", None)),
        check_vma=False,
    )
```

```python
import functools

import jax
import jax.numpy as jnp
from jax import lax
from jax.experimental import pallas as pl
from jax.experimental.pallas import tpu as pltpu
from jax.sharding import PartitionSpec as P

BLK = 128
TPR = 6
NB = 8
OV = 512
NLOC = 1024
K = 128
TAIL = K * K // OV
CHEB_CENTER = 2.5
CHEB_HALF = 1.5
RHO_FIRST = CHEB_HALF / CHEB_CENTER
RHO_SECOND = 1.0 / (2.0 * CHEB_CENTER / CHEB_HALF - RHO_FIRST)
F32 = jnp.float32
BF16 = jnp.bfloat16
VMEM = pl.BlockSpec(memory_space=pltpu.VMEM)
SMEM = pl.BlockSpec(memory_space=pltpu.SMEM)
HBM = pl.BlockSpec(memory_space=pltpu.HBM)
NT = (((1,), (1,)), ((), ()))
STEPS = ((2, 0), (2, 1), (1, 0), (1, 1), (0, 1), (3, 0), (3, 1), (0, 0))
EARLY = 6
INSIDE = STEPS.index((0, 0))
ACROSS = STEPS.index((0, 1))
NEAR_2 = STEPS.index((1, 0))
FAR_2 = STEPS.index((1, 1))
REST = tuple(i for i in range(8) if i not in (INSIDE, ACROSS))
ROWS = 2 * K + TAIL


def permute(block, target):
    n = lax.axis_size("sub")
    return lax.ppermute(block, "sub", [(i, target(i) % n) for i in range(n)])


def swapped(block, power, colour):
    o = 1 << power
    return permute(block, lambda i: i + o if (i // o) % 2 == colour else i - o)


def core_swap(block):
    return permute(block, lambda i: i ^ 1)


def both_ways(block, chips):
    return permute(block, lambda i: i + 2 * chips if i % 2 == 0 else i - 2 * chips)


def bit(me, power):
    return lax.rem(lax.div(me, 1 << power), 2)


def slot_of(step, me):
    power, colour = STEPS[step]
    side = 1 - bit(me, 0) if power == 1 else bit(me, power)
    return power + 4 * (side if colour == 0 else 1 - side)


def near_step_is_first(power, me):
    return power == 1 or bit(me, power) != bit(me, 0)


def split(x):
    hi = x.astype(BF16)
    return hi, (x - hi.astype(F32)).astype(BF16)


def column(diag_ref, b):
    return jnp.broadcast_to(diag_ref[b : b + 1, :], (BLK, BLK)).T


def tile_row(cols_ref, tiles_ref, v_ref, b):
    acc = None
    for t in range(TPR * b, TPR * (b + 1)):
        rows = pl.ds(pl.multiple_of(cols_ref[t] * BLK, BLK), BLK)
        term = jnp.dot(tiles_ref[t], v_ref[rows, :], preferred_element_type=F32)
        acc = term if acc is None else acc + term
    return acc


def picks(margin_ref, slot):
    rows = margin_ref[pl.ds(slot, 1), :]
    ids = lax.broadcasted_iota(jnp.int32, (NLOC, OV), 0)
    return jnp.where(ids == rows, 1.0, 0.0).astype(BF16)


def prepare(cols_in, z_in, tiles_in, diag_in, rhs_in, margin_in, *rest):
    inside_ref, own_ref, coarse_ref, zit = rest[:4]
    cols_ref, z_ref, tiles_ref, diag_ref, rhs_ref, margin_ref, images, sems = rest[4:]
    me = lax.axis_index("sub")
    pairs = [(z_in, z_ref), (rhs_in, rhs_ref), (cols_in, cols_ref), (diag_in, diag_ref)]
    pairs += [(tiles_in.at[pl.ds(TPR * b, TPR)], tiles_ref.at[pl.ds(TPR * b, TPR)]) for b in range(NB)]
    pairs += [(margin_in, margin_ref)]
    copies = [pltpu.make_async_copy(src, dst, sems.at[i]) for i, (src, dst) in enumerate(pairs)]
    for copy in copies:
        copy.start()
    copies[0].wait()
    for b in range(NB):
        rows = slice(b * BLK, (b + 1) * BLK)
        zit[:K, rows] = z_ref[rows, :].T
    for copy in copies[1:4]:
        copy.wait()
    coarse = jnp.dot(zit[:K, :], rhs_ref[...], preferred_element_type=F32)
    coarse_ref[...] = coarse
    first = (coarse / CHEB_CENTER).astype(BF16)
    for copy in copies[4:]:
        copy.wait()
    for b in range(NB):
        rows = slice(b * BLK, (b + 1) * BLK)
        z = z_ref[rows, :]
        image = (column(diag_ref, b) * z.astype(F32) + tile_row(cols_ref, tiles_ref, z_ref, b)).astype(BF16)
        zit[K:, rows] = image.T
        images[rows, :] = image
    for i, step in enumerate((INSIDE, ACROSS)):
        gather(inside_ref, i * ROWS, zit, margin_ref, slot_of(step, me), first)
    own_ref[...] = jnp.dot(zit[:K, :], images[...], preferred_element_type=F32)


def gather(out, at, zit, margin_ref, slot, first):
    rows = jnp.dot(zit[...], picks(margin_ref, slot), preferred_element_type=F32).astype(BF16)
    out[at : at + 2 * K, :] = rows
    for q in range(OV // K):
        out[at + 2 * K : at + ROWS, q * K : (q + 1) * K] = first[q * TAIL : (q + 1) * TAIL, :]


def prepare_rest(margin_ref, zit, coarse_ref, *payloads):
    me = lax.axis_index("sub")
    first = (coarse_ref[...] / CHEB_CENTER).astype(BF16)
    for step, out in zip(REST, payloads):
        gather(out, 0, zit, margin_ref, slot_of(step, me), first)


dot = functools.partial(jnp.dot, preferred_element_type=F32)


def pair_block(mine, theirs, adj_ref, step, me):
    block = lax.dot_general(mine[: 2 * K, :], theirs[: 2 * K, :], NT, preferred_element_type=F32)
    weight = adj_ref[0, slot_of(step, me)].astype(F32) * 0.5
    return split((block[:K, K:] + block[K:, :K]) * weight)


def take_first(theirs, v_ref, at):
    for q in range(OV // K):
        v_ref[at + q * TAIL : at + (q + 1) * TAIL, :] = theirs[2 * K :, q * K : (q + 1) * K]


def iterate_early(adj_ref, own_ref, coarse_ref, *rest):
    mine, theirs = rest[:EARLY], rest[EARLY : 2 * EARLY]
    ehi_ref, elo_ref, image_ref, v_ref = rest[2 * EARLY :]
    me = lax.axis_index("sub")
    ehi_ref[:, :K], elo_ref[:, :K] = split(own_ref[...])
    v_ref[:K, :], first_lo = split(coarse_ref[...] / CHEB_CENTER)
    for step in range(EARLY):
        at = (step + 1) * K
        ehi_ref[:, at : at + K], elo_ref[:, at : at + K] = pair_block(mine[step], theirs[step], adj_ref, step, me)
        take_first(theirs[step], v_ref, at)
    image_ref[...] = dot(ehi_ref[...], v_ref[...]) + dot(elo_ref[...], v_ref[...]) + dot(ehi_ref[:, :K], first_lo)


def iterate(adj_ref, coarse_ref, image_ref, *rest):
    late = 8 - EARLY
    mine, theirs = rest[:late], rest[late : 2 * late]
    ehi_ref, elo_ref, send_ref, v_ref = rest[2 * late :]
    me = lax.axis_index("sub")
    coarse = coarse_ref[...]
    first = coarse / CHEB_CENTER
    for i in range(late):
        at = i * K
        ehi_ref[:, at : at + K], elo_ref[:, at : at + K] = pair_block(mine[i], theirs[i], adj_ref, EARLY + i, me)
        take_first(theirs[i], v_ref, at)
    image = image_ref[...] + (dot(ehi_ref[...], v_ref[...]) + dot(elo_ref[...], v_ref[...]))
    second = RHO_SECOND * RHO_FIRST * first + (2.0 * RHO_SECOND / CHEB_HALF) * (coarse - image)
    send_ref[:, :K], send_ref[:, K:] = split(first + second)


def arrive(adj_ref, margin_ref, slot, basis, coeffs):
    corr = lax.dot_general(coeffs, basis, (((0,), (0,)), ((), ())), preferred_element_type=F32).astype(BF16)
    corr = corr * adj_ref[0, slot].astype(BF16)
    return lax.dot_general(picks(margin_ref, slot), corr, NT, preferred_element_type=F32)


def corrections(adj_ref, pieces):
    out = []
    for slot, basis, coeffs in pieces:
        corr = lax.dot_general(coeffs, basis, (((0,), (0,)), ((), ())), preferred_element_type=F32).astype(BF16)
        out.append(corr * adj_ref[0, slot].astype(BF16))
    return out


def scatter(margin_ref, slots, corrs):
    onehot = jnp.concatenate([picks(margin_ref, slot) for slot in slots], axis=1)
    return lax.dot_general(onehot, jnp.concatenate(corrs, axis=1), NT, preferred_element_type=F32)


def merge_chip(adj_ref, z_ref, margin_ref, send_ref, other_ref, basis_ref, out_ref):
    me = lax.axis_index("sub")
    local = dot(z_ref[...], send_ref[:, :K]).astype(BF16).astype(F32)
    out_ref[...] = local + arrive(adj_ref, margin_ref, slot_of(INSIDE, me), basis_ref[:K, :], other_ref[:, :K])


def pick_basis(power, a_ref, b_ref, near, me):
    a, b = STEPS.index((power, 0)), STEPS.index((power, 1))
    take_a = near_step_is_first(power, me) == near
    if isinstance(take_a, bool):
        return (a_ref if take_a else b_ref)[:K, :], slot_of(a if take_a else b, me), a if take_a else b
    slot = jnp.where(take_a, slot_of(a, me), slot_of(b, me))
    return jnp.where(take_a, a_ref[:K, :], b_ref[:K, :]), slot, jnp.where(take_a, a, b)


def merge_near(power, adj_ref, margin_ref, summed_ref, vectors_ref, a_ref, b_ref, out_ref):
    me = lax.axis_index("sub")
    basis, slot, _ = pick_basis(power, a_ref, b_ref, True, me)
    out_ref[...] = summed_ref[...] + arrive(adj_ref, margin_ref, slot, basis, vectors_ref[:K, :K])


def merge_next(adj_ref, margin_ref, summed_ref, vectors_ref, across_ref, a_ref, b_ref, out_ref):
    me = lax.axis_index("sub")
    basis, slot, _ = pick_basis(1, a_ref, b_ref, True, me)
    slots = (slot_of(ACROSS, me), slot)
    corrs = corrections(adj_ref, ((slots[0], across_ref[:K, :], vectors_ref[K:, :K]), (slot, basis, vectors_ref[:K, :K])))
    out_ref[...] = summed_ref[...] + scatter(margin_ref, slots, corrs)


def finish(cols_ref, adj_ref, tiles_ref, diag_ref, rhs_ref, margin_ref, coarse_ref, ehi_early, elo_early, ehi_late, elo_late, summed_ref, send_ref, other_ref, one_ref, two_ref, four_ref, far_ref, *rest):
    theirs = rest[:8]
    fine_ref, coarse_out, v_ref, merged = rest[8:]
    me = lax.axis_index("sub")
    pieces = []
    v_ref[:K, :] = send_ref[...]
    v_ref[(INSIDE + 1) * K : (INSIDE + 2) * K, :] = other_ref[...]
    v_ref[(ACROSS + 1) * K : (ACROSS + 2) * K, :] = one_ref[K:, :]
    for power, ref in ((1, one_ref), (2, two_ref), (3, four_ref)):
        far = far_ref[(power - 1) * K : power * K, :]
        a, b = STEPS.index((power, 0)), STEPS.index((power, 1))
        basis, slot, step = pick_basis(power, theirs[a], theirs[b], False, me)
        pieces.append((slot, basis, far[:, :K]))
        near_step = a + b - step
        v_ref[pl.ds(pl.multiple_of((step + 1) * K, K), K), :] = far
        v_ref[pl.ds(pl.multiple_of((near_step + 1) * K, K), K), :] = ref[:K, :]
    added = scatter(margin_ref, [p[0] for p in pieces], corrections(adj_ref, pieces))
    merged[...] = (summed_ref[...] + added).astype(BF16)
    early, late = slice(0, (EARLY + 1) * K), slice((EARLY + 1) * K, 9 * K)
    both = dot(ehi_early[...], v_ref[early, :]) + dot(ehi_late[...], v_ref[late, :])
    small = dot(elo_early[...], v_ref[early, :K]) + dot(elo_late[...], v_ref[late, :K])
    coarse_out[...] = coarse_ref[...] - (both[:, :K] + (both[:, K:] + small))
    for b in range(NB):
        rows = slice(b * BLK, (b + 1) * BLK)
        image = column(diag_ref, b) * merged[rows, :].astype(F32) + tile_row(cols_ref, tiles_ref, merged, b)
        fine_ref[rows, :] = (rhs_ref[rows, :].astype(F32) - image).astype(BF16)


def arr(shape, dtype):
    return jax.ShapeDtypeStruct(shape, dtype)


def call(kernel, name, in_specs, outs, scratch, flops, limit=32, moved=2**20):
    return pl.pallas_call(
        kernel,
        name=name,
        in_specs=in_specs,
        out_specs=[VMEM] * len(outs),
        out_shape=outs,
        scratch_shapes=scratch,
        compiler_params=pltpu.CompilerParams(vmem_limit_bytes=limit * 1024 * 1024),
        cost_estimate=pl.CostEstimate(flops=flops, bytes_accessed=moved, transcendentals=0),
    )


def per_device(deflation, op_tiles, tile_cols, diag_coef, fine_rhs, adjacency, margin_rows):
    diag = diag_coef.reshape(NB, BLK)
    margin = margin_rows[0]
    sent_inside, own, coarse, zit = call(
        prepare,
        "prepare",
        [HBM] * 6,
        [arr((2 * ROWS, OV), BF16)] + [arr((K, K), F32)] * 2 + [arr((2 * K, NLOC), BF16)],
        [
            pltpu.SMEM((TPR * NB,), jnp.int32),
            pltpu.VMEM((NLOC, K), BF16),
            pltpu.VMEM((TPR * NB, BLK, BLK), BF16),
            pltpu.VMEM((NB, BLK), F32),
            pltpu.VMEM((NLOC, K), BF16),
            pltpu.VMEM((8, OV), jnp.int32),
            pltpu.VMEM((NLOC, K), BF16),
            pltpu.SemaphoreType.DMA((NB + 5,)),
        ],
        3 * 10**9,
    )(*(pltpu.with_memory_space_constraint(x, pltpu.HBM) for x in (tile_cols, deflation, op_tiles, diag, fine_rhs, margin)))
    others = call(
        prepare_rest,
        "prepare_rest",
        [VMEM] * 3,
        [arr((ROWS, OV), BF16)] * len(REST),
        [],
        8 * 10**9,
    )(margin, zit, coarse)
    payloads = [None] * 8
    for step, block in zip(REST, others):
        payloads[step] = block
    payloads[INSIDE], payloads[ACROSS] = sent_inside[:ROWS], sent_inside[ROWS:]
    theirs = [None] * 8
    inside = core_swap(sent_inside)
    theirs[STEPS.index((2, 0))] = swapped(payloads[STEPS.index((2, 0))], 2, 0)
    theirs[STEPS.index((2, 1))] = swapped(payloads[STEPS.index((2, 1))], 2, 1)
    forth = both_ways(jnp.concatenate([payloads[FAR_2], inside[ROWS:]]), 1)
    theirs[FAR_2] = both_ways(payloads[NEAR_2], -1)
    theirs[STEPS.index((3, 0))] = swapped(payloads[STEPS.index((3, 0))], 3, 0)
    theirs[STEPS.index((3, 1))] = swapped(payloads[STEPS.index((3, 1))], 3, 1)
    theirs[INSIDE], theirs[NEAR_2], theirs[ACROSS] = inside[:ROWS], forth[:ROWS], forth[ROWS:]
    early = (EARLY + 1) * K
    ehi_early, elo_early, image = call(
        iterate_early,
        "iterate_early",
        [SMEM] + [VMEM] * (2 + 2 * EARLY),
        [arr((K, early), BF16)] * 2 + [arr((K, K), F32)],
        [pltpu.VMEM((early, K), BF16)],
        10**9,
    )(adjacency, own, coarse, *payloads[:EARLY], *theirs[:EARLY])
    late = (8 - EARLY) * K
    ehi_late, elo_late, send = call(
        iterate,
        "iterate",
        [SMEM] + [VMEM] * (2 + 2 * (8 - EARLY)),
        [arr((K, late), BF16)] * 2 + [arr((K, 2 * K), BF16)],
        [pltpu.VMEM((late, K), BF16)],
        10**9,
    )(adjacency, coarse, image, *payloads[EARLY:], *theirs[EARLY:])
    other = core_swap(send)
    pair = jnp.concatenate([send, other])
    one, two, four = (both_ways(pair, chips) for chips in (1, 2, 4))
    summed = call(
        merge_chip, "merge_chip", [SMEM] + [VMEM] * 5, [arr((NLOC, K), F32)], [], 10**9
    )(adjacency, deflation, margin, send, other, theirs[INSIDE])[0]
    near = {power: [theirs[STEPS.index((power, colour))] for colour in (0, 1)] for power in (1, 2, 3)}
    for power, vectors in ((3, four), (2, two)):
        summed = call(
            functools.partial(merge_near, power), f"merge_{power}", [SMEM] + [VMEM] * 5, [arr((NLOC, K), F32)], [], 1, moved=1
        )(adjacency, margin, summed, vectors, *near[power])[0]
    one_late, summed = lax.optimization_barrier((one, summed))
    hand_over = jnp.concatenate([one_late[K:], two[K:], four[K:]])
    far = core_swap(hand_over)
    summed = call(merge_next, "merge_next", [SMEM] + [VMEM] * 6, [arr((NLOC, K), F32)], [], 10**9)(
        adjacency, margin, summed, one, theirs[ACROSS], *near[1]
    )[0]
    return tuple(
        call(
            finish,
            "finish",
            [SMEM] * 2 + [VMEM] * 24,
            [arr((NLOC, K), BF16), arr((K, K), F32)],
            [pltpu.VMEM((9 * K, 2 * K), BF16), pltpu.VMEM((NLOC, K), BF16)],
            3 * 10**9,
        )(tile_cols, adjacency, op_tiles, diag, fine_rhs, margin, coarse, ehi_early, elo_early, ehi_late, elo_late, summed, send, other, one, two, four, far, *theirs)
    )


def solution(mesh):
    return jax.shard_map(
        per_device,
        mesh=mesh,
        in_specs=(P("sub", None), P("sub", None, None), P("sub"), P("sub"), P("sub", None), P("sub", None), P("sub", None, None)),
        out_specs=(P("sub", None), P("sub", None)),
        check_vma=False,
    )
```

```python
import functools

import jax
import jax.numpy as jnp
from jax import lax
from jax.experimental import pallas as pl
from jax.experimental.pallas import tpu as pltpu
from jax.sharding import PartitionSpec as P

BLK = 128
TPR = 6
NB = 8
OV = 512
NLOC = 1024
K = 128
TAIL = K * K // OV
CHEB_CENTER = 2.5
CHEB_HALF = 1.5
RHO_FIRST = CHEB_HALF / CHEB_CENTER
RHO_SECOND = 1.0 / (2.0 * CHEB_CENTER / CHEB_HALF - RHO_FIRST)
F32 = jnp.float32
BF16 = jnp.bfloat16
VMEM = pl.BlockSpec(memory_space=pltpu.VMEM)
SMEM = pl.BlockSpec(memory_space=pltpu.SMEM)
HBM = pl.BlockSpec(memory_space=pltpu.HBM)
NT = (((1,), (1,)), ((), ()))
STEPS = ((2, 0), (2, 1), (1, 0), (1, 1), (0, 1), (3, 0), (3, 1), (0, 0))
EARLY = 6
INSIDE = STEPS.index((0, 0))
ACROSS = STEPS.index((0, 1))
NEAR_2 = STEPS.index((1, 0))
FAR_2 = STEPS.index((1, 1))
REST = tuple(i for i in range(8) if i not in (INSIDE, ACROSS))
ROWS = 2 * K + TAIL


def permute(block, target):
    n = lax.axis_size("sub")
    return lax.ppermute(block, "sub", [(i, target(i) % n) for i in range(n)])


def swapped(block, power, colour):
    o = 1 << power
    return permute(block, lambda i: i + o if (i // o) % 2 == colour else i - o)


def core_swap(block):
    return permute(block, lambda i: i ^ 1)


def both_ways(block, chips):
    return permute(block, lambda i: i + 2 * chips if i % 2 == 0 else i - 2 * chips)


def bit(me, power):
    return lax.rem(lax.div(me, 1 << power), 2)


def slot_of(step, me):
    power, colour = STEPS[step]
    side = 1 - bit(me, 0) if power == 1 else bit(me, power)
    return power + 4 * (side if colour == 0 else 1 - side)


def near_step_is_first(power, me):
    return power == 1 or bit(me, power) != bit(me, 0)


def split(x):
    hi = x.astype(BF16)
    return hi, (x - hi.astype(F32)).astype(BF16)


def column(diag_ref, b):
    return jnp.broadcast_to(diag_ref[b : b + 1, :], (BLK, BLK)).T


def tile_row(cols_ref, tiles_ref, v_ref, b):
    acc = None
    for t in range(TPR * b, TPR * (b + 1)):
        rows = pl.ds(pl.multiple_of(cols_ref[t] * BLK, BLK), BLK)
        term = jnp.dot(tiles_ref[t], v_ref[rows, :], preferred_element_type=F32)
        acc = term if acc is None else acc + term
    return acc


def picks(margin_ref, slot):
    rows = margin_ref[pl.ds(slot, 1), :]
    ids = lax.broadcasted_iota(jnp.int32, (NLOC, OV), 0)
    return jnp.where(ids == rows, 1.0, 0.0).astype(BF16)


def prepare(cols_in, z_in, tiles_in, diag_in, rhs_in, margin_in, *rest):
    inside_ref, own_ref, coarse_ref, zit = rest[:4]
    cols_ref, z_ref, tiles_ref, diag_ref, rhs_ref, margin_ref, images, sems = rest[4:]
    me = lax.axis_index("sub")
    pairs = [(z_in, z_ref), (rhs_in, rhs_ref), (cols_in, cols_ref), (diag_in, diag_ref)]
    pairs += [(tiles_in.at[pl.ds(TPR * b, TPR)], tiles_ref.at[pl.ds(TPR * b, TPR)]) for b in range(NB)]
    pairs += [(margin_in, margin_ref)]
    copies = [pltpu.make_async_copy(src, dst, sems.at[i]) for i, (src, dst) in enumerate(pairs)]
    for copy in copies:
        copy.start()
    copies[0].wait()
    for b in range(NB):
        rows = slice(b * BLK, (b + 1) * BLK)
        zit[:K, rows] = z_ref[rows, :].T
    for copy in copies[1:4]:
        copy.wait()
    coarse = jnp.dot(zit[:K, :], rhs_ref[...], preferred_element_type=F32)
    coarse_ref[...] = coarse
    first = (coarse / CHEB_CENTER).astype(BF16)
    for copy in copies[4:]:
        copy.wait()
    for b in range(NB):
        rows = slice(b * BLK, (b + 1) * BLK)
        z = z_ref[rows, :]
        image = (column(diag_ref, b) * z.astype(F32) + tile_row(cols_ref, tiles_ref, z_ref, b)).astype(BF16)
        zit[K:, rows] = image.T
        images[rows, :] = image
    for i, step in enumerate((INSIDE, ACROSS)):
        gather(inside_ref, i * ROWS, zit, margin_ref, slot_of(step, me), first)
    own_ref[...] = jnp.dot(zit[:K, :], images[...], preferred_element_type=F32)


def gather(out, at, zit, margin_ref, slot, first):
    rows = jnp.dot(zit[...], picks(margin_ref, slot), preferred_element_type=F32).astype(BF16)
    out[at : at + 2 * K, :] = rows
    for q in range(OV // K):
        out[at + 2 * K : at + ROWS, q * K : (q + 1) * K] = first[q * TAIL : (q + 1) * TAIL, :]


def prepare_rest(margin_ref, zit, coarse_ref, *payloads):
    me = lax.axis_index("sub")
    first = (coarse_ref[...] / CHEB_CENTER).astype(BF16)
    for step, out in zip(REST, payloads):
        gather(out, 0, zit, margin_ref, slot_of(step, me), first)


dot = functools.partial(jnp.dot, preferred_element_type=F32)


def pair_block(mine, theirs, adj_ref, step, me):
    block = lax.dot_general(mine[: 2 * K, :], theirs[: 2 * K, :], NT, preferred_element_type=F32)
    weight = adj_ref[0, slot_of(step, me)].astype(F32) * 0.5
    return split((block[:K, K:] + block[K:, :K]) * weight)


def take_first(theirs, v_ref, at):
    for q in range(OV // K):
        v_ref[at + q * TAIL : at + (q + 1) * TAIL, :] = theirs[2 * K :, q * K : (q + 1) * K]


def iterate_early(adj_ref, own_ref, coarse_ref, *rest):
    mine, theirs = rest[:EARLY], rest[EARLY : 2 * EARLY]
    ehi_ref, elo_ref, image_ref, v_ref = rest[2 * EARLY :]
    me = lax.axis_index("sub")
    ehi_ref[:, :K], elo_ref[:, :K] = split(own_ref[...])
    v_ref[:K, :], first_lo = split(coarse_ref[...] / CHEB_CENTER)
    for step in range(EARLY):
        at = (step + 1) * K
        ehi_ref[:, at : at + K], elo_ref[:, at : at + K] = pair_block(mine[step], theirs[step], adj_ref, step, me)
        take_first(theirs[step], v_ref, at)
    image_ref[...] = dot(ehi_ref[...], v_ref[...]) + dot(elo_ref[...], v_ref[...]) + dot(ehi_ref[:, :K], first_lo)


def iterate(adj_ref, coarse_ref, image_ref, *rest):
    late = 8 - EARLY
    mine, theirs = rest[:late], rest[late : 2 * late]
    ehi_ref, elo_ref, send_ref, v_ref = rest[2 * late :]
    me = lax.axis_index("sub")
    coarse = coarse_ref[...]
    first = coarse / CHEB_CENTER
    for i in range(late):
        at = i * K
        ehi_ref[:, at : at + K], elo_ref[:, at : at + K] = pair_block(mine[i], theirs[i], adj_ref, EARLY + i, me)
        take_first(theirs[i], v_ref, at)
    image = image_ref[...] + (dot(ehi_ref[...], v_ref[...]) + dot(elo_ref[...], v_ref[...]))
    second = RHO_SECOND * RHO_FIRST * first + (2.0 * RHO_SECOND / CHEB_HALF) * (coarse - image)
    send_ref[:, :K], send_ref[:, K:] = split(first + second)


def arrive(adj_ref, margin_ref, slot, basis, coeffs):
    corr = lax.dot_general(coeffs, basis, (((0,), (0,)), ((), ())), preferred_element_type=F32).astype(BF16)
    corr = corr * adj_ref[0, slot].astype(BF16)
    return lax.dot_general(picks(margin_ref, slot), corr, NT, preferred_element_type=F32)


def corrections(adj_ref, pieces):
    out = []
    for slot, basis, coeffs in pieces:
        corr = lax.dot_general(coeffs, basis, (((0,), (0,)), ((), ())), preferred_element_type=F32).astype(BF16)
        out.append(corr * adj_ref[0, slot].astype(BF16))
    return out


def scatter(margin_ref, slots, corrs):
    onehot = jnp.concatenate([picks(margin_ref, slot) for slot in slots], axis=1)
    return lax.dot_general(onehot, jnp.concatenate(corrs, axis=1), NT, preferred_element_type=F32)


def merge_chip(adj_ref, z_ref, margin_ref, send_ref, other_ref, basis_ref, out_ref):
    me = lax.axis_index("sub")
    local = dot(z_ref[...], send_ref[:, :K]).astype(BF16).astype(F32)
    out_ref[...] = local + arrive(adj_ref, margin_ref, slot_of(INSIDE, me), basis_ref[:K, :], other_ref[:, :K])


def pick_basis(power, a_ref, b_ref, near, me):
    a, b = STEPS.index((power, 0)), STEPS.index((power, 1))
    take_a = near_step_is_first(power, me) == near
    if isinstance(take_a, bool):
        return (a_ref if take_a else b_ref)[:K, :], slot_of(a if take_a else b, me), a if take_a else b
    slot = jnp.where(take_a, slot_of(a, me), slot_of(b, me))
    return jnp.where(take_a, a_ref[:K, :], b_ref[:K, :]), slot, jnp.where(take_a, a, b)


def merge_near(adj_ref, margin_ref, summed_ref, two_ref, four_ref, a2_ref, b2_ref, a3_ref, b3_ref, out_ref):
    me = lax.axis_index("sub")
    pieces = []
    for power, vectors_ref, a_ref, b_ref in ((2, two_ref, a2_ref, b2_ref), (3, four_ref, a3_ref, b3_ref)):
        basis, slot, _ = pick_basis(power, a_ref, b_ref, True, me)
        pieces.append((slot, basis, vectors_ref[:K, :K]))
    added = scatter(margin_ref, [p[0] for p in pieces], corrections(adj_ref, pieces))
    out_ref[...] = summed_ref[...] + added


def merge_next(adj_ref, margin_ref, summed_ref, vectors_ref, across_ref, a_ref, b_ref, out_ref):
    me = lax.axis_index("sub")
    basis, slot, _ = pick_basis(1, a_ref, b_ref, True, me)
    slots = (slot_of(ACROSS, me), slot)
    corrs = corrections(adj_ref, ((slots[0], across_ref[:K, :], vectors_ref[K:, :K]), (slot, basis, vectors_ref[:K, :K])))
    out_ref[...] = summed_ref[...] + scatter(margin_ref, slots, corrs)


def finish(cols_ref, adj_ref, tiles_ref, diag_ref, rhs_ref, margin_ref, coarse_ref, ehi_early, elo_early, ehi_late, elo_late, summed_ref, send_ref, other_ref, one_ref, two_ref, four_ref, far_ref, *rest):
    theirs = rest[:8]
    fine_ref, coarse_out, v_ref, merged = rest[8:]
    me = lax.axis_index("sub")
    pieces = []
    v_ref[:K, :] = send_ref[...]
    v_ref[(INSIDE + 1) * K : (INSIDE + 2) * K, :] = other_ref[...]
    v_ref[(ACROSS + 1) * K : (ACROSS + 2) * K, :] = one_ref[K:, :]
    for power, ref in ((1, one_ref), (2, two_ref), (3, four_ref)):
        far = far_ref[(power - 1) * K : power * K, :]
        a, b = STEPS.index((power, 0)), STEPS.index((power, 1))
        basis, slot, step = pick_basis(power, theirs[a], theirs[b], False, me)
        pieces.append((slot, basis, far[:, :K]))
        near_step = a + b - step
        v_ref[pl.ds(pl.multiple_of((step + 1) * K, K), K), :] = far
        v_ref[pl.ds(pl.multiple_of((near_step + 1) * K, K), K), :] = ref[:K, :]
    added = scatter(margin_ref, [p[0] for p in pieces], corrections(adj_ref, pieces))
    merged[...] = (summed_ref[...] + added).astype(BF16)
    early, late = slice(0, (EARLY + 1) * K), slice((EARLY + 1) * K, 9 * K)
    both = dot(ehi_early[...], v_ref[early, :]) + dot(ehi_late[...], v_ref[late, :])
    small = dot(elo_early[...], v_ref[early, :K]) + dot(elo_late[...], v_ref[late, :K])
    coarse_out[...] = coarse_ref[...] - (both[:, :K] + (both[:, K:] + small))
    for b in range(NB):
        rows = slice(b * BLK, (b + 1) * BLK)
        image = column(diag_ref, b) * merged[rows, :].astype(F32) + tile_row(cols_ref, tiles_ref, merged, b)
        fine_ref[rows, :] = (rhs_ref[rows, :].astype(F32) - image).astype(BF16)


def arr(shape, dtype):
    return jax.ShapeDtypeStruct(shape, dtype)


def call(kernel, name, in_specs, outs, scratch, flops, limit=32, moved=2**20):
    return pl.pallas_call(
        kernel,
        name=name,
        in_specs=in_specs,
        out_specs=[VMEM] * len(outs),
        out_shape=outs,
        scratch_shapes=scratch,
        compiler_params=pltpu.CompilerParams(vmem_limit_bytes=limit * 1024 * 1024),
        cost_estimate=pl.CostEstimate(flops=flops, bytes_accessed=moved, transcendentals=0),
    )


def per_device(deflation, op_tiles, tile_cols, diag_coef, fine_rhs, adjacency, margin_rows):
    diag = diag_coef.reshape(NB, BLK)
    margin = margin_rows[0]
    sent_inside, own, coarse, zit = call(
        prepare,
        "prepare",
        [HBM] * 6,
        [arr((2 * ROWS, OV), BF16)] + [arr((K, K), F32)] * 2 + [arr((2 * K, NLOC), BF16)],
        [
            pltpu.SMEM((TPR * NB,), jnp.int32),
            pltpu.VMEM((NLOC, K), BF16),
            pltpu.VMEM((TPR * NB, BLK, BLK), BF16),
            pltpu.VMEM((NB, BLK), F32),
            pltpu.VMEM((NLOC, K), BF16),
            pltpu.VMEM((8, OV), jnp.int32),
            pltpu.VMEM((NLOC, K), BF16),
            pltpu.SemaphoreType.DMA((NB + 5,)),
        ],
        3 * 10**9,
    )(*(pltpu.with_memory_space_constraint(x, pltpu.HBM) for x in (tile_cols, deflation, op_tiles, diag, fine_rhs, margin)))
    others = call(
        prepare_rest,
        "prepare_rest",
        [VMEM] * 3,
        [arr((ROWS, OV), BF16)] * len(REST),
        [],
        8 * 10**9,
    )(margin, zit, coarse)
    payloads = [None] * 8
    for step, block in zip(REST, others):
        payloads[step] = block
    payloads[INSIDE], payloads[ACROSS] = sent_inside[:ROWS], sent_inside[ROWS:]
    theirs = [None] * 8
    inside = core_swap(sent_inside)
    theirs[STEPS.index((2, 0))] = swapped(payloads[STEPS.index((2, 0))], 2, 0)
    theirs[STEPS.index((2, 1))] = swapped(payloads[STEPS.index((2, 1))], 2, 1)
    forth = both_ways(jnp.concatenate([payloads[FAR_2], inside[ROWS:]]), 1)
    theirs[FAR_2] = both_ways(payloads[NEAR_2], -1)
    theirs[STEPS.index((3, 0))] = swapped(payloads[STEPS.index((3, 0))], 3, 0)
    theirs[STEPS.index((3, 1))] = swapped(payloads[STEPS.index((3, 1))], 3, 1)
    theirs[INSIDE], theirs[NEAR_2], theirs[ACROSS] = inside[:ROWS], forth[:ROWS], forth[ROWS:]
    early = (EARLY + 1) * K
    ehi_early, elo_early, image = call(
        iterate_early,
        "iterate_early",
        [SMEM] + [VMEM] * (2 + 2 * EARLY),
        [arr((K, early), BF16)] * 2 + [arr((K, K), F32)],
        [pltpu.VMEM((early, K), BF16)],
        10**9,
    )(adjacency, own, coarse, *payloads[:EARLY], *theirs[:EARLY])
    late = (8 - EARLY) * K
    ehi_late, elo_late, send = call(
        iterate,
        "iterate",
        [SMEM] + [VMEM] * (2 + 2 * (8 - EARLY)),
        [arr((K, late), BF16)] * 2 + [arr((K, 2 * K), BF16)],
        [pltpu.VMEM((late, K), BF16)],
        10**9,
    )(adjacency, coarse, image, *payloads[EARLY:], *theirs[EARLY:])
    other = core_swap(send)
    pair = jnp.concatenate([send, other])
    one, two, four = (both_ways(pair, chips) for chips in (1, 2, 4))
    summed = call(
        merge_chip, "merge_chip", [SMEM] + [VMEM] * 5, [arr((NLOC, K), F32)], [], 10**9
    )(adjacency, deflation, margin, send, other, theirs[INSIDE])[0]
    near = {power: [theirs[STEPS.index((power, colour))] for colour in (0, 1)] for power in (1, 2, 3)}
    summed = call(merge_near, "merge_near", [SMEM] + [VMEM] * 8, [arr((NLOC, K), F32)], [], 1, moved=1)(
        adjacency, margin, summed, two, four, *near[2], *near[3]
    )[0]
    one_late, summed = lax.optimization_barrier((one, summed))
    hand_over = jnp.concatenate([one_late[K:], two[K:], four[K:]])
    far = core_swap(hand_over)
    summed = call(merge_next, "merge_next", [SMEM] + [VMEM] * 6, [arr((NLOC, K), F32)], [], 10**9)(
        adjacency, margin, summed, one, theirs[ACROSS], *near[1]
    )[0]
    return tuple(
        call(
            finish,
            "finish",
            [SMEM] * 2 + [VMEM] * 24,
            [arr((NLOC, K), BF16), arr((K, K), F32)],
            [pltpu.VMEM((9 * K, 2 * K), BF16), pltpu.VMEM((NLOC, K), BF16)],
            3 * 10**9,
        )(tile_cols, adjacency, op_tiles, diag, fine_rhs, margin, coarse, ehi_early, elo_early, ehi_late, elo_late, summed, send, other, one, two, four, far, *theirs)
    )


def solution(mesh):
    return jax.shard_map(
        per_device,
        mesh=mesh,
        in_specs=(P("sub", None), P("sub", None, None), P("sub"), P("sub"), P("sub", None), P("sub", None), P("sub", None, None)),
        out_specs=(P("sub", None), P("sub", None)),
        check_vma=False,
    )
```
